256 devices in a mesh: gy: 32 (over z_hi, y, core), gx: 8 (over x, z_lo).
Axes of the slice: x: 4, y: 4, z: 8 (z_hi: 4, z_lo: 2; z = z_hi * 2 + z_lo), core: 2. Of those that a mesh axis runs over, the one named last changes fastest.
Arguments:
- second_section_map: bfloat16 [1024, 512, 256], P('gy', 'gx'), may hold values from -6 to 6
- convolution_weight: bfloat16 [3, 3, 256, 512], replicated, may hold values from -0.125 to 0.125
- convolution_bias: float32 [512], replicated, may hold values from -3 to 3
- downsampler_gain: float32 [512], replicated, may hold values from 0.25 to 1.75
- downsampler_shift: float32 [512], replicated, may hold values from -2 to 2
- prenorm_gains: float32 [2, 512], replicated, may hold values from 0.25 to 1.75
- prenorm_shifts: float32 [2, 512], replicated, may hold values from -2 to 2
- query_key_value_weight: bfloat16 [2, 512, 1536], replicated, may hold values from -2 to 2
- query_key_value_bias: float32 [2, 1536], replicated, may hold values from -2 to 2
- relative_offset_bias: float32 [2, 16, 49], replicated, may hold values from -4 to 4
- output_projection_weight: bfloat16 [2, 512, 512], replicated, may hold values from -0.25 to 0.25
- output_projection_bias: float32 [2, 512], replicated, may hold values from -2 to 2
Outputs:
- features: bfloat16 [512, 256, 512], P('gy', 'gx')
The draws below stay inside these ranges and needn't reach their ends.
All inputs are finite; a program needn't handle non-finite values.
Results may differ from the reference program's by a relative error of at most 0.019.
Values may be sent and summed in bfloat16 or wider, within the bound.
No kernel may reach another device: no remote copies, remote signals or barrier semaphores. Data moves between devices by JAX's collectives and lax.ppermute only.
A program may use at most 128 MiB of HBM per device.

```python
import jax
import jax.numpy as jnp
from jax import lax

C2 = 256
C3 = 512
HEADS = 16
KERNEL = 7
SECOND_DILATION = 8
TILE_R = 16
ROWS = 512
COLS = 256
ROWS2 = 1024
COLS2 = 512


def draw_query_key_value_weight(key, part):
    base = jax.random.normal(key, (2, C3, 3 * C3), jnp.float32)
    base = jnp.clip(base, -4.0, 4.0) * C3 ** (-0.5)
    return jnp.clip(base, -2.0, 2.0).astype(jnp.bfloat16)


def block_levels(stream_key, shape, split, smallest, largest):
    gain = 1.0
    for dim, blocks in split:
        heights = jax.random.uniform(jax.random.fold_in(jax.random.fold_in(stream_key, 6), dim), (blocks,), jnp.float32, smallest / len(split), largest / len(split))
        gain = gain * jnp.repeat(jnp.exp(heights), shape[dim] // blocks).reshape((-1,) + (1,) * (len(shape) - 1 - dim))
    return gain


def normal_values(rng, dims, deviation, reach, split=(), dtype=jnp.bfloat16):
    drawn = deviation * jax.random.normal(rng, dims, jnp.float32)
    if split:
        drawn = drawn * block_levels(rng, dims, split, -0.22, 0.18)
    return jnp.clip(drawn, -reach, reach).astype(dtype)


def setup_inputs(seed: int = 0) -> dict:
    keys = jax.random.split(jax.random.key(seed), 13)
    second_section_map = normal_values(keys[0], (ROWS2, COLS2, C2), 1.0, 6.0, ((0, 32), (1, 8)))
    convolution_weight = normal_values(keys[1], (3, 3, C2, C3), (9 * C2) ** -0.5, 0.125)
    convolution_bias = normal_values(keys[2], (C3,), 0.5, 3.0, (), jnp.float32)
    downsampler_gain = jnp.clip(1.0 + 0.15 * jax.random.normal(keys[3], (C3,), jnp.float32), 0.25, 1.75)
    downsampler_shift = normal_values(keys[4], (C3,), 0.3, 2.0, (), jnp.float32)
    prenorm_gains = jnp.clip(1.0 + 0.15 * jax.random.normal(keys[5], (2, C3), jnp.float32), 0.25, 1.75)
    prenorm_shifts = normal_values(keys[6], (2, C3), 0.3, 2.0, (), jnp.float32)
    query_key_value_weight = draw_query_key_value_weight(jax.random.fold_in(keys[12], 71), 0)
    query_key_value_bias = normal_values(keys[8], (2, 3 * C3), 0.3, 2.0, (), jnp.float32)
    relative_offset_bias = normal_values(keys[9], (2, HEADS, KERNEL * KERNEL), 1.0, 4.0, (), jnp.float32)
    output_projection_weight = normal_values(keys[10], (2, C3, C3), C3 ** -0.5, 0.25)
    output_projection_bias = normal_values(keys[11], (2, C3), 0.3, 2.0, (), jnp.float32)
    return {"second_section_map": second_section_map, "convolution_weight": convolution_weight, "convolution_bias": convolution_bias, "downsampler_gain": downsampler_gain, "downsampler_shift": downsampler_shift, "prenorm_gains": prenorm_gains, "prenorm_shifts": prenorm_shifts, "query_key_value_weight": query_key_value_weight, "query_key_value_bias": query_key_value_bias, "relative_offset_bias": relative_offset_bias, "output_projection_weight": output_projection_weight, "output_projection_bias": output_projection_bias}


def layer_norm(values, norm_gains, norm_add):
    average = lax.optimization_barrier(jnp.mean(values, axis=-1, keepdims=True))
    centred = values - average
    spread = lax.optimization_barrier(jnp.mean(centred * centred, axis=-1, keepdims=True))
    return centred * lax.rsqrt(spread + 1e-05) * norm_gains + norm_add

def attend(queries, keys_ext, values_ext, valid_ext, rel_row, dilation):
    height, width, channels = queries.shape
    reach_rows = 3 * dilation
    head_count = rel_row.shape[0]
    head_size = channels // head_count
    factor = head_size ** (-0.5)
    q_heads = queries.astype(jnp.float32).reshape(height, width, head_count, head_size)
    scores = []
    for row_step in range(KERNEL):
        for col_step in range(KERNEL):
            row_at = reach_rows + dilation * (row_step - KERNEL // 2)
            col_at = reach_rows + dilation * (col_step - KERNEL // 2)
            shifted = keys_ext[row_at:row_at + height, col_at:col_at + width].astype(jnp.float32)
            shifted = shifted.reshape(height, width, head_count, head_size)
            logits = lax.optimization_barrier(jnp.sum(q_heads * shifted, axis=-1)) * factor + rel_row[:, row_step * KERNEL + col_step]
            inside = valid_ext[row_at:row_at + height, col_at:col_at + width]
            scores.append(jnp.where(inside[:, :, None], logits, -1e+30))
    stacked = jnp.stack(scores)
    row_peak = lax.optimization_barrier(jnp.max(stacked, axis=0))
    exponent = jnp.exp(stacked - row_peak)
    weights = (exponent / lax.optimization_barrier(jnp.sum(exponent, axis=0))).astype(jnp.bfloat16)
    summed = jnp.zeros((height, width, head_count, head_size), jnp.float32)
    position = 0
    for row_step in range(KERNEL):
        for col_step in range(KERNEL):
            row_at = reach_rows + dilation * (row_step - KERNEL // 2)
            col_at = reach_rows + dilation * (col_step - KERNEL // 2)
            picked = values_ext[row_at:row_at + height, col_at:col_at + width].astype(jnp.float32)
            picked = picked.reshape(height, width, head_count, head_size)
            summed = summed + weights[position].astype(jnp.float32)[:, :, :, None] * picked
            position = position + 1
    return summed.reshape(height, width, channels).astype(jnp.bfloat16)

def attention_sublayer(token_grid, prenorm_gains, prenorm_shifts, query_key_value_weight, query_key_value_bias, relative_offset_bias, output_projection_weight, output_projection_bias, layer_id, dilation):
    normed = layer_norm(token_grid.astype(jnp.float32), prenorm_gains[layer_id], prenorm_shifts[layer_id]).astype(jnp.bfloat16)
    flat = normed.reshape(ROWS * COLS, C3)
    projected = jnp.dot(flat, query_key_value_weight[layer_id], preferred_element_type=jnp.float32) + query_key_value_bias[layer_id]
    projected = projected.astype(jnp.bfloat16).reshape(ROWS, COLS, 3 * C3)
    queries = projected[:, :, :C3]
    reach_rows = 3 * dilation
    margin = ((reach_rows, reach_rows), (reach_rows, reach_rows), (0, 0))
    keys_pad = jnp.pad(projected[:, :, C3:2 * C3], margin)
    values_pad = jnp.pad(projected[:, :, 2 * C3:], margin)
    valid_pad = jnp.pad(jnp.ones((ROWS, COLS), jnp.bool_), reach_rows)
    span = TILE_R + 2 * reach_rows

    def one_block(start):
        q_block = lax.dynamic_slice_in_dim(queries, start, TILE_R, 0)
        k_block = lax.dynamic_slice_in_dim(keys_pad, start, span, 0)
        v_block = lax.dynamic_slice_in_dim(values_pad, start, span, 0)
        m_block = lax.dynamic_slice_in_dim(valid_pad, start, span, 0)
        return attend(q_block, k_block, v_block, m_block, relative_offset_bias[layer_id], dilation)
    starts = (jnp.arange(ROWS // TILE_R) * TILE_R).astype(jnp.int32)
    attended = lax.map(one_block, starts).reshape(ROWS * COLS, C3)
    branch = jnp.dot(attended, output_projection_weight[layer_id], preferred_element_type=jnp.float32) + output_projection_bias[layer_id]
    updated = token_grid.astype(jnp.float32).reshape(ROWS * COLS, C3) + branch
    return updated.astype(jnp.bfloat16).reshape(ROWS, COLS, C3)

def reference(second_section_map, convolution_weight, convolution_bias, downsampler_gain, downsampler_shift, prenorm_gains, prenorm_shifts, query_key_value_weight, query_key_value_bias, relative_offset_bias, output_projection_weight, output_projection_bias):
    framed = jnp.pad(second_section_map, ((1, 0), (1, 0), (0, 0)))
    summed = jnp.zeros((ROWS * COLS, C3), jnp.float32)
    for offset_r in range(3):
        for offset_c in range(3):
            tapped = framed[offset_r:offset_r + ROWS2:2, offset_c:offset_c + COLS2:2]
            summed = summed + jnp.dot(tapped.reshape(ROWS * COLS, C2), convolution_weight[offset_r, offset_c], preferred_element_type=jnp.float32)
    token_grid = layer_norm(summed + convolution_bias, downsampler_gain, downsampler_shift).astype(jnp.bfloat16).reshape(ROWS, COLS, C3)
    token_grid = attention_sublayer(token_grid, prenorm_gains, prenorm_shifts, query_key_value_weight, query_key_value_bias, relative_offset_bias, output_projection_weight, output_projection_bias, 0, 1)
    token_grid = attention_sublayer(token_grid, prenorm_gains, prenorm_shifts, query_key_value_weight, query_key_value_bias, relative_offset_bias, output_projection_weight, output_projection_bias, 1, SECOND_DILATION)
    return token_grid
```

```python
import functools

import jax
import jax.numpy as jnp
import ml_dtypes
import numpy as np
from jax import lax
from jax.experimental import pallas as pl
from jax.experimental.pallas import tpu as pltpu
from jax.sharding import Mesh, PartitionSpec as P

F32 = jnp.float32
BF16 = jnp.bfloat16
KERNEL = 7
HALF = 3
NEG = -1e30
LOG2E = 1.4426950408889634
TR, TC = 16, 32
C2, C3 = 256, 512
HEADS, HD = 16, 32
GROUP = 8
DIL = 8
PAIRS = 11
PT = 80
NTOK = PAIRS * PT
EPS = 1e-5
VMEM_LIMIT = 56 * 1024 * 1024


def pair_slots():
    out = []
    for rp in range(2):
        for c in range(16):
            out.append((rp * 16 + c, rp, c))
        for c in range(16, 22):
            out.append((32 + rp * 6 + c - 16, rp, c))
        for c in range(22, 38):
            out.append((48 + rp * 16 + c - 22, rp, c))
    return out


def pick_matrix():
    pick = np.zeros((3 * PT, 160), np.float32)
    for b in range(3):
        for slot, rp, c in pair_slots():
            col = 2 * c + b - 7
            if col < 0:
                k = 128 + 16 * rp + col + 8
            elif col < 64:
                k = 64 * rp + col
            else:
                k = 128 + 16 * rp + 8 + col - 64
            pick[b * PT + slot, k] = 1
    return pick


def near_keys():
    rows = np.full((2, 256), -99, np.int32)
    cols = np.full((2, 256), -99, np.int32)
    for half in range(2):
        for j in range(5):
            for slot, rp, c in pair_slots():
                at = slot - 32 * half
                if 0 <= at < 48:
                    rows[half, 48 * j + at] = 2 * j + rp
                    cols[half, 48 * j + at] = c - 16 * half
    return rows, cols


def query_matrix():
    rows, cols = near_keys()
    sel = np.zeros((2, 64, 256), np.float32)
    for half in range(2):
        for k in range(256):
            r, c = rows[half, k] - 3, cols[half, k] - 3
            if 0 <= r < 4 and 0 <= c < 16:
                sel[half, r * 16 + c, k] = 1
    return sel


def offset_onehot(qr, qc, kr, kc):
    dr = kr[None, :] - qr[:, None]
    dc = kc[None, :] - qc[:, None]
    near = (np.abs(dr) <= HALF) & (np.abs(dc) <= HALF)
    pos = (dr + HALF) * KERNEL + dc + HALF
    hot = (pos[None] == np.arange(49)[:, None, None]) & near[None]
    return hot.astype(np.float32), near


def near_tables():
    rows, cols = near_keys()
    q = np.arange(64)
    made = [offset_onehot(q // 16 + 3, q % 16 + 3, rows[h], cols[h]) for h in range(2)]
    return np.stack([m[0] for m in made], 1), np.stack([m[1] for m in made])


def far_tables():
    q = np.arange(64)
    k = np.arange(256)
    qr = (q % 8) // 4
    qc = 4 * (q // 8) + q % 4
    return offset_onehot(qr + 3, qc, k // 32, k % 32)


def send_matrix():
    perm = np.zeros((512, 512), np.float32)
    for m in range(4):
        for h in range(2):
            for qr in range(4):
                for qc in range(16):
                    row, col = 4 * m + qr, 16 * h + qc
                    dst = ((row % 8) * 8 + col % 8) * 8 + (row // 8) * 4 + col // 8
                    perm[dst, (m * 2 + h) * 64 + qr * 16 + qc] = 1
    return perm


def far_key_matrix():
    sel = np.zeros((64, 128), np.float32)
    for src in range(2):
        for gx in range(8):
            for a in range(2):
                for b in range(4):
                    if (src == 0) == (a == 1):
                        rp = src
                        sel[rp * 32 + gx * 4 + b, src * 64 + gx * 8 + a * 4 + b] = 1
    return sel


def back_matrix():
    sel = np.zeros((64, 64), np.float32)
    for j in range(8):
        for a in range(2):
            for b in range(4):
                sel[a * 32 + b * 8 + j, j * 8 + a * 4 + b] = 1
    return sel


def bf(x):
    return jnp.asarray(x.astype(ml_dtypes.bfloat16))


def norm(v, gain, shift):
    mean = jnp.mean(v, axis=-1, keepdims=True)
    d = v - mean
    var = jnp.mean(d * d, axis=-1, keepdims=True)
    return d * lax.rsqrt(var + EPS) * gain + shift


def attend_block(q, k, v, table_ref, table_at, extra):
    lane = lax.broadcasted_iota(jnp.int32, (1, 256), 1) // HD
    outs = []
    for g in range(HEADS // GROUP):
        at = slice(256 * g, 256 * g + 256)
        qg, kg, vg = q[:, at], k[:, at], v[:, at]
        stacked = jnp.concatenate(
            [qg * (lane == h).astype(BF16) for h in range(GROUP)], axis=0
        )
        s = lax.dot_general(stacked, kg, (((1,), (1,)), ((), ())), preferred_element_type=F32)
        s = s * (HD**-0.5 * LOG2E) + (table_ref[table_at + (g,)] + extra)
        peak = jnp.max(s, axis=-1, keepdims=True)
        p = jnp.exp2(s - peak)
        total = jnp.sum(p, axis=-1, keepdims=True)
        o = jnp.dot(p.astype(BF16), vg, preferred_element_type=F32) * (1.0 / total)
        acc = jnp.zeros((64, 256), F32)
        for h in range(GROUP):
            acc = jnp.where(lane == h, o[64 * h : 64 * h + 64], acc)
        outs.append(acc)
    return jnp.concatenate(outs, axis=1)


def near_kernel(
    flag_ref, up, own, down, rim, pick, wconv, bconv, gain0, shift0, gain1, shift1, wqkv, bqkv,
    table, extra, qsel, wout, bout, send, out, cat, x0s, ys, ks, vs, yq, xq, qs, att,
):
    flag = flag_ref[0].astype(BF16)

    def main_row(e):
        if e < 7:
            row = up[e]
            return row * flag if e == 6 else row
        return own[e - 7] if e < 39 else down[e - 39]

    def rim_row(e):
        return rim[e] * flag if e == 6 else rim[e]

    for p in range(PAIRS):
        for a in range(3):
            e0, e1 = 4 * p + a, 4 * p + a + 2
            rows = jnp.concatenate([main_row(e0), main_row(e1), rim_row(e0), rim_row(e1)], axis=0)
            got = jnp.dot(pick[...], rows, preferred_element_type=F32).astype(BF16)
            for b in range(3):
                cat[PT * p : PT * p + PT, 256 * (3 * a + b) : 256 * (3 * a + b) + 256] = got[
                    PT * b : PT * b + PT
                ]
    conv = jnp.dot(cat[...], wconv[...], preferred_element_type=F32) + bconv[...]
    x0 = norm(conv, gain0[...], shift0[...]).astype(BF16)
    y = norm(x0.astype(F32), gain1[...], shift1[...]).astype(BF16)
    x0s[...] = x0.reshape(PAIRS, PT, C3)
    ys[...] = y.reshape(PAIRS, PT, C3)
    kv = jnp.dot(y, wqkv[:, C3:], preferred_element_type=F32) + bqkv[:, C3:]
    ks[...] = kv[:, :C3].astype(BF16).reshape(PAIRS, PT, C3)
    vs[...] = kv[:, C3:].astype(BF16).reshape(PAIRS, PT, C3)

    def window(ref, m, h):
        part = ref[pl.ds(2 * m, 5), 32 * h : 32 * h + 48, :].reshape(240, C3)
        return jnp.concatenate([part, part[:16]], axis=0)

    for m in range(4):
        for h in range(2):
            at = slice((2 * m + h) * 64, (2 * m + h) * 64 + 64)
            sel = qsel[h]
            yq[at] = jnp.dot(sel, window(ys, m, h), preferred_element_type=F32).astype(BF16)
            xq[at] = jnp.dot(sel, window(x0s, m, h), preferred_element_type=F32)
    qs[...] = (jnp.dot(yq[...], wqkv[:, :C3], preferred_element_type=F32) + bqkv[:, :C3]).astype(BF16)

    def block(m, _):
        for h in range(2):
            at = pl.ds(pl.multiple_of((2 * m + h) * 64, 64), 64)
            o = attend_block(
                qs[at], window(ks, m, h), window(vs, m, h), table, (h,), extra[pl.ds(2 * m + h, 1), :]
            )
            att[at] = o.astype(BF16)
        return 0

    lax.fori_loop(0, 4, block, 0)
    x1 = jnp.dot(att[...], wout[...], preferred_element_type=F32) + bout[...] + xq[...]
    out[...] = jnp.dot(send[...], x1.astype(BF16), preferred_element_type=F32).astype(BF16)


def far_kernel(
    above, own, below, gain, shift, wqkv, bqkv, ksel, table, extra, wout, bout, out, ys, yk, ks, vs, qs, att
):
    for ref, at, n in ((above, 0, 128), (own, 128, 512), (below, 640, 128)):
        ys[at : at + n] = norm(ref[...].astype(F32), gain[...], shift[...]).astype(BF16)
    for j in range(PAIRS):
        yk[64 * j : 64 * j + 64] = jnp.dot(
            ksel[...], ys[64 * j : 64 * j + 128], preferred_element_type=F32
        ).astype(BF16)
    kv = jnp.dot(yk[...], wqkv[:, C3:], preferred_element_type=F32) + bqkv[:, C3:]
    ks[...] = kv[:, :C3].astype(BF16)
    vs[...] = kv[:, C3:].astype(BF16)
    qs[...] = (
        jnp.dot(ys[128:640], wqkv[:, :C3], preferred_element_type=F32) + bqkv[:, :C3]
    ).astype(BF16)

    def block(m, _):
        at = pl.ds(pl.multiple_of(m * 64, 64), 64)
        keys = pl.ds(pl.multiple_of(m * 64, 64), 256)
        o = attend_block(qs[at], ks[keys], vs[keys], table, (), extra[pl.ds(m, 1), :])
        att[at] = o.astype(BF16)
        return 0

    lax.fori_loop(0, 8, block, 0)
    x2 = jnp.dot(att[...], wout[...], preferred_element_type=F32) + bout[...]
    out[...] = (x2 + own[...].astype(F32)).astype(BF16)


def back_kernel(got, sel, out):
    for i in range(8):
        rows = jnp.dot(sel[...], got[64 * i : 64 * i + 64], preferred_element_type=F32).astype(BF16)
        out[i] = rows[:32]
        out[8 + i] = rows[32:]


def call(kernel, out_shape, scratch, args, smem=0):
    specs = [pl.BlockSpec(memory_space=pltpu.SMEM)] * smem
    specs += [pl.BlockSpec(memory_space=pltpu.VMEM)] * (len(args) - smem)
    return pl.pallas_call(
        kernel,
        out_shape=jax.ShapeDtypeStruct(out_shape, BF16),
        in_specs=specs,
        out_specs=pl.BlockSpec(memory_space=pltpu.VMEM),
        scratch_shapes=[pltpu.VMEM(s, t) for s, t in scratch],
        compiler_params=pltpu.CompilerParams(vmem_limit_bytes=VMEM_LIMIT),
    )(*args)


def per_device(
    zsize, isize, xsize,
    fmap, wconv, bconv, gain0, shift0, gains, shifts, wqkv, bqkv, rel, wout, bout,
):
    zi, ii, xi = lax.axis_index("gz"), lax.axis_index("gi"), lax.axis_index("gx")
    ysize = zsize * isize
    yi = zi * isize + ii

    def shifted(x, dy, dx):
        pairs = [
            (y * xsize + c, ((y + dy) % ysize) * xsize + (c + dx) % xsize)
            for y in range(ysize)
            for c in range(xsize)
        ]
        return lax.ppermute(x, ("gz", "gi", "gx"), pairs)

    up = shifted(fmap[25:], 1, 0)
    down = shifted(fmap[:6], -1, 0)

    def tables(hot, near, layer):
        t = jnp.einsum("ho,o...->h...", rel[layer], jnp.asarray(hot), precision=lax.Precision.HIGHEST)
        return jnp.where(jnp.asarray(near)[None], t * LOG2E, NEG)

    hot0, near0 = near_tables()
    table0 = tables(hot0, near0, 0).transpose(1, 0, 2, 3).reshape(2, 2, GROUP * 64, 256)
    hot1, near1 = far_tables()
    table1 = tables(hot1, near1, 1).reshape(2, GROUP * 64, 256)

    krow, kcol = near_keys()
    rows0 = yi * TR - 3 + np.repeat(np.arange(4) * 4, 2)[:, None] + np.tile(krow, (4, 1))
    cols0 = xi * TC - 3 + np.tile(np.arange(2) * 16, 4)[:, None] + np.tile(kcol, (4, 1))
    inside0 = (rows0 >= 0) & (rows0 < ysize * TR) & (cols0 >= 0) & (cols0 < xsize * TC)
    extra0 = jnp.where(inside0, 0.0, NEG).astype(F32)
    rows1 = zi * 16 - 3 + 2 * np.arange(8)[:, None] + np.arange(256)[None] // 32
    extra1 = jnp.where((rows1 >= 0) & (rows1 < zsize * 16), 0.0, NEG).astype(F32)

    def strip(at):
        return jnp.concatenate([up[:, at], fmap[:, at], down[:, at]], axis=0)

    left = shifted(strip(slice(56, 64)), 0, 1)
    right = shifted(strip(slice(0, 8)), 0, -1)
    rim = jnp.concatenate([jnp.where(xi == 0, jnp.zeros_like(left), left), right], axis=1)
    flag = jnp.where(yi == 0, 0.0, 1.0).astype(F32).reshape(1)

    row = lambda v: v.reshape(1, -1)
    x1 = call(
        near_kernel,
        (512, C3),
        [
            ((NTOK, 9 * C2), BF16), ((PAIRS, PT, C3), BF16), ((PAIRS, PT, C3), BF16),
            ((PAIRS, PT, C3), BF16), ((PAIRS, PT, C3), BF16), ((512, C3), BF16), ((512, C3), F32),
            ((512, C3), BF16), ((512, C3), BF16),
        ],
        [
            flag, up, fmap, down, rim, bf(pick_matrix()), wconv.reshape(9 * C2, C3), row(bconv),
            row(gain0), row(shift0), row(gains[0]), row(shifts[0]), wqkv[0], row(bqkv[0]), table0,
            extra0, bf(query_matrix()), wout[0], row(bout[0]), bf(send_matrix()),
        ],
        smem=1,
    )
    got = lax.all_to_all(x1.reshape(64, 8, C3), ("gi", "gx"), 0, 0).reshape(512, C3)
    step = isize
    above = shifted(got[384:], step, 0)
    below = shifted(got[:128], -step, 0)
    x2 = call(
        far_kernel,
        (512, C3),
        [
            ((768, C3), BF16), ((704, C3), BF16), ((704, C3), BF16), ((704, C3), BF16),
            ((512, C3), BF16), ((512, C3), BF16),
        ],
        [
            above, got, below, row(gains[1]), row(shifts[1]), wqkv[1], row(bqkv[1]),
            bf(far_key_matrix()), table1, extra1, wout[1], row(bout[1]),
        ],
    )
    back = lax.all_to_all(x2.reshape(64, 8, C3), ("gi", "gx"), 0, 0).reshape(512, C3)
    return call(back_kernel, (TR, TC, C3), [], [back, bf(back_matrix())])


def solution(mesh):
    gy, gx = mesh.shape["gy"], mesh.shape["gx"]
    inner = Mesh(mesh.devices.reshape(gy // 8, 8, gx), ("gz", "gi", "gx"))
    tile = P(("gz", "gi"), "gx", None)
    placed = (tile,) + (P(),) * 11
    return jax.shard_map(
        functools.partial(per_device, gy // 8, 8, gx),
        mesh=inner,
        in_specs=placed,
        out_specs=tile,
        check_vma=False,
    )
```

```python
import functools

import jax
import jax.numpy as jnp
import ml_dtypes
import numpy as np
from jax import lax
from jax.experimental import pallas as pl
from jax.experimental.pallas import tpu as pltpu
from jax.sharding import Mesh, PartitionSpec as P

F32 = jnp.float32
BF16 = jnp.bfloat16
KERNEL = 7
HALF = 3
NEG = -1e30
LOG2E = 1.4426950408889634
TR, TC = 16, 32
C2, C3 = 256, 512
HEADS, HD = 16, 32
GROUP = 8
DIL = 8
PAIRS = 11
PT = 80
NTOK = PAIRS * PT
EPS = 1e-5
VMEM_LIMIT = 36 * 1024 * 1024


def pair_slots():
    out = []
    for rp in range(2):
        for c in range(16):
            out.append((rp * 16 + c, rp, c))
        for c in range(16, 22):
            out.append((32 + rp * 8 + c - 16, rp, c))
        for c in range(22, 38):
            out.append((48 + rp * 16 + c - 22, rp, c))
    return out


def pick_matrix():
    pick = np.zeros((3 * PT, 160), np.float32)
    for b in range(3):
        for slot, rp, c in pair_slots():
            col = 2 * c + b - 7
            if col < 0:
                k = 128 + 8 * rp + col + 8
            elif col < 64:
                k = 64 * rp + col
            else:
                k = 144 + 8 * rp + col - 64
            pick[b * PT + slot, k] = 1
    return pick


def near_keys():
    rows = np.full((2, 256), -99, np.int32)
    cols = np.full((2, 256), -99, np.int32)
    for half in range(2):
        for j in range(5):
            for slot, rp, c in pair_slots():
                at = slot - 32 * half
                if 0 <= at < 48:
                    rows[half, 48 * j + at] = 2 * j + rp
                    cols[half, 48 * j + at] = c - 16 * half
    return rows, cols


def query_matrix():
    rows, cols = near_keys()
    sel = np.zeros((2, 64, 256), np.float32)
    for half in range(2):
        for k in range(256):
            r, c = rows[half, k] - 3, cols[half, k] - 3
            if 0 <= r < 4 and 0 <= c < 16:
                sel[half, r * 16 + c, k] = 1
    return sel


def near_patterns():
    rows, cols = near_keys()
    hot = np.zeros((49, 2, 2, 4, 256), np.float32)
    code = np.zeros((2, 64, 256), np.int32)
    for half in range(2):
        for k in range(256):
            if rows[half, k] < 0:
                continue
            wide = (cols[half, k] < 16) if half == 0 else (cols[half, k] >= 6)
            for q in range(64):
                dr, dc = rows[half, k] - q // 16, cols[half, k] - q % 16
                if 0 <= dr < 7 and 0 <= dc < 7:
                    part = 0 if wide else 1
                    code[half, q, k] = 1 + part
                    hot[dr * 7 + dc, half, part, q // 16, (k - q % 16) % 256] = 1
    return hot.reshape(49, 4096), code


def far_patterns():
    hot = np.zeros((49, 2, 256), np.float32)
    code = np.zeros((64, 256), np.int32)
    for q in range(64):
        gx, a, b = q // 8, q % 8 // 4, q % 4
        for k in range(256):
            dr, dc = k // 32 - a, k % 32 - (4 * gx + b) + 3
            if 0 <= dr < 7 and 0 <= dc < 7:
                code[q, k] = 1
                hot[dr * 7 + dc, a, (k - 4 * gx - 4 * a - b) % 256] = 1
    return hot.reshape(49, 512), code


def send_matrix():
    perm = np.zeros((512, 512), np.float32)
    for m in range(4):
        for h in range(2):
            for qr in range(4):
                for qc in range(16):
                    row, col = 4 * m + qr, 16 * h + qc
                    dst = ((row % 8) * 8 + col % 8) * 8 + (row // 8) * 4 + col // 8
                    perm[dst, (m * 2 + h) * 64 + qr * 16 + qc] = 1
    return perm


def far_key_matrix():
    sel = np.zeros((64, 128), np.float32)
    for src in range(2):
        for gx in range(8):
            for a in range(2):
                for b in range(4):
                    if (src == 0) == (a == 1):
                        rp = src
                        sel[rp * 32 + gx * 4 + b, src * 64 + gx * 8 + a * 4 + b] = 1
    return sel


def back_matrix():
    sel = np.zeros((64, 64), np.float32)
    for j in range(8):
        for a in range(2):
            for b in range(4):
                sel[a * 32 + b * 8 + j, j * 8 + a * 4 + b] = 1
    return sel


def bf(x):
    return jnp.asarray(x.astype(ml_dtypes.bfloat16))


def norm(v, gain, shift):
    mean = jnp.mean(v, axis=-1, keepdims=True)
    d = v - mean
    var = jnp.mean(d * d, axis=-1, keepdims=True)
    return d * lax.rsqrt(var + EPS) * gain + shift


def attend_block(q, k, v, table, extra):
    lane = lax.broadcasted_iota(jnp.int32, (1, 256), 1) // HD
    outs = []
    for g in range(HEADS // GROUP):
        at = slice(256 * g, 256 * g + 256)
        qg, kg, vg = q[:, at], k[:, at], v[:, at]
        stacked = jnp.concatenate(
            [qg * (lane == h).astype(BF16) for h in range(GROUP)], axis=0
        )
        s = lax.dot_general(stacked, kg, (((1,), (1,)), ((), ())), preferred_element_type=F32)
        s = s * (HD**-0.5 * LOG2E) + (table(g) + extra)
        peak = jnp.max(s, axis=-1, keepdims=True)
        p = jnp.exp2(s - peak)
        total = jnp.sum(p, axis=-1, keepdims=True)
        o = jnp.dot(p.astype(BF16), vg, preferred_element_type=F32) * (1.0 / total)
        acc = jnp.zeros((64, 256), F32)
        for h in range(GROUP):
            acc = jnp.where(lane == h, o[64 * h : 64 * h + 64], acc)
        outs.append(acc)
    return jnp.concatenate(outs, axis=1)


def table_kernel(rel, hot0, code0, hot1, code1, t0, t1):
    def spread(r, hot):
        hi = r.astype(BF16)
        mid = (r - hi.astype(F32)).astype(BF16)
        lo = (r - hi.astype(F32) - mid.astype(F32)).astype(BF16)
        dot = functools.partial(jnp.dot, preferred_element_type=F32)
        return (dot(hi, hot[...]) + dot(mid, hot[...]) + dot(lo, hot[...])) * LOG2E

    e0 = spread(rel[0], hot0)
    e1 = spread(rel[1], hot1)
    for h in range(HEADS):
        for half in range(2):
            for qr in range(4):
                part = []
                for i in range(2):
                    at = ((half * 2 + i) * 4 + qr) * 256
                    one = jnp.broadcast_to(e0[h : h + 1, at : at + 256], (16, 256))
                    part.append(pltpu.roll(one, 0, 1, stride=1, stride_axis=0))
                code = code0[half, 16 * qr : 16 * qr + 16]
                row = h % GROUP * 64 + 16 * qr
                t0[half, h // GROUP, row : row + 16] = jnp.where(
                    code == 1, part[0], jnp.where(code == 2, part[1], NEG)
                )
        two = jnp.concatenate(
            [jnp.broadcast_to(e1[h : h + 1, 256 * a : 256 * a + 256], (4, 256)) for a in range(2)], axis=0
        )
        for gx in range(8):
            row = h % GROUP * 64 + 8 * gx
            t1[h // GROUP, row : row + 8] = jnp.where(
                code1[8 * gx : 8 * gx + 8] == 1, pltpu.roll(two, 4 * gx, 1, stride=1, stride_axis=0), NEG
            )


def near_kernel(
    pos, own_hbm, wconv_hbm, wqkv_hbm, wout_hbm, send_hbm, up, down, left, right, pick, bconv, gain0,
    shift0, gains, shifts, bqkv, table, krow, kcol, qsel, bout, out, cat, x0s, ys, ks, vs, yq, xq, qs,
    att, own, wconv, wqkv, wout, send, extra, sems,
):
    copies = [
        pltpu.make_async_copy(src, dst, sems.at[i])
        for i, (src, dst) in enumerate(
            (
                (own_hbm, own), (wconv_hbm, wconv), (wqkv_hbm.at[0], wqkv), (wout_hbm.at[0], wout),
                (send_hbm, send),
            )
        )
    ]
    for copy in copies:
        copy.start()
    yi, xi, ysize, xsize = pos[0], pos[1], pos[3], pos[4]
    top = jnp.where(yi == 0, 0.0, 1.0).astype(BF16)
    side = jnp.where(xi == 0, 0.0, 1.0).astype(BF16)
    rows, cols = krow[...] + yi * TR, kcol[...] + xi * TC
    inside = (rows >= 0) & (rows < ysize * TR) & (cols >= 0) & (cols < xsize * TC)
    extra[...] = jnp.where(inside, 0.0, NEG)
    copies[0].wait()

    def main_row(e):
        if e < 7:
            row = up[e]
            return row * top if e == 6 else row
        return own[e - 7] if e < 39 else down[e - 39]

    def left_row(e):
        row = left[e] * side
        return row * top if e == 6 else row

    def right_row(e):
        return right[e] * top if e == 6 else right[e]

    for p in range(PAIRS):
        for a in range(3):
            e0, e1 = 4 * p + a, 4 * p + a + 2
            rows = jnp.concatenate(
                [main_row(e0), main_row(e1), left_row(e0), left_row(e1), right_row(e0), right_row(e1)],
                axis=0,
            )
            got = jnp.dot(pick[...], rows, preferred_element_type=F32).astype(BF16)
            for b in range(3):
                cat[PT * p : PT * p + PT, 256 * (3 * a + b) : 256 * (3 * a + b) + 256] = got[
                    PT * b : PT * b + PT
                ]
    copies[1].wait()
    conv = jnp.dot(cat[...], wconv[...], preferred_element_type=F32) + bconv[...]
    x0 = norm(conv, gain0[...], shift0[...]).astype(BF16)
    y = norm(x0.astype(F32), gains[0:1], shifts[0:1]).astype(BF16)
    x0s[...] = x0.reshape(PAIRS, PT, C3)
    ys[...] = y.reshape(PAIRS, PT, C3)
    copies[2].wait()
    kv = jnp.dot(y, wqkv[:, C3:], preferred_element_type=F32) + bqkv[0:1, C3:]
    ks[...] = kv[:, :C3].astype(BF16).reshape(PAIRS, PT, C3)
    vs[...] = kv[:, C3:].astype(BF16).reshape(PAIRS, PT, C3)

    def window(ref, m, h):
        part = ref[pl.ds(2 * m, 5), 32 * h : 32 * h + 48, :].reshape(240, C3)
        return jnp.concatenate([part, part[:16]], axis=0)

    for m in range(4):
        for h in range(2):
            at = slice((2 * m + h) * 64, (2 * m + h) * 64 + 64)
            sel = qsel[h]
            yq[at] = jnp.dot(sel, window(ys, m, h), preferred_element_type=F32).astype(BF16)
            xq[at] = jnp.dot(sel, window(x0s, m, h), preferred_element_type=F32)
    qs[...] = (
        jnp.dot(yq[...], wqkv[:, :C3], preferred_element_type=F32) + bqkv[0:1, :C3]
    ).astype(BF16)

    def block(m, _):
        for h in range(2):
            at = pl.ds(pl.multiple_of((2 * m + h) * 64, 64), 64)
            o = attend_block(
                qs[at], window(ks, m, h), window(vs, m, h), lambda g: table[h, g],
                extra[pl.ds(2 * m + h, 1), :],
            )
            att[at] = o.astype(BF16)
        return 0

    lax.fori_loop(0, 4, block, 0)
    copies[3].wait()
    copies[4].wait()
    x1 = jnp.dot(att[...], wout[...], preferred_element_type=F32) + bout[0:1] + xq[...]
    out[...] = jnp.dot(send[...], x1.astype(BF16), preferred_element_type=F32).astype(BF16)


def far_kernel(
    pos, wqkv_hbm, wout_hbm, above, own, below, gains, shifts, bqkv, ksel, table, bout, out, ys, yk, ks,
    vs, qs, att, wqkv, wout, sems,
):
    copies = [
        pltpu.make_async_copy(src, dst, sems.at[i])
        for i, (src, dst) in enumerate(((wqkv_hbm.at[1], wqkv), (wout_hbm.at[1], wout)))
    ]
    for copy in copies:
        copy.start()
    zi, zsize = pos[2], pos[5]
    for ref, at, n in ((above, 0, 128), (own, 128, 512), (below, 640, 128)):
        ys[at : at + n] = norm(ref[...].astype(F32), gains[1:2], shifts[1:2]).astype(BF16)
    for j in range(PAIRS):
        yk[64 * j : 64 * j + 64] = jnp.dot(
            ksel[...], ys[64 * j : 64 * j + 128], preferred_element_type=F32
        ).astype(BF16)
    copies[0].wait()
    kv = jnp.dot(yk[...], wqkv[:, C3:], preferred_element_type=F32) + bqkv[1:2, C3:]
    ks[...] = kv[:, :C3].astype(BF16)
    vs[...] = kv[:, C3:].astype(BF16)
    qs[...] = (
        jnp.dot(ys[128:640], wqkv[:, :C3], preferred_element_type=F32) + bqkv[1:2, :C3]
    ).astype(BF16)
    key_row = lax.broadcasted_iota(jnp.int32, (1, 256), 1) // 32 - 3

    def block(i, _):
        for u in range(2):
            m = 2 * i + u
            row = key_row + (16 * zi + 2 * m)
            extra = jnp.where((row >= 0) & (row < 16 * zsize), 0.0, NEG)
            at = pl.ds(pl.multiple_of(m * 64, 64), 64)
            keys = pl.ds(pl.multiple_of(m * 64, 64), 256)
            o = attend_block(qs[at], ks[keys], vs[keys], lambda g: table[g], extra)
            att[at] = o.astype(BF16)
        return 0

    lax.fori_loop(0, 4, block, 0)
    copies[1].wait()
    x2 = jnp.dot(att[...], wout[...], preferred_element_type=F32) + bout[1:2]
    out[...] = (x2 + own[...].astype(F32)).astype(BF16)


def back_kernel(got, sel, out):
    for i in range(8):
        rows = jnp.dot(sel[...], got[64 * i : 64 * i + 64], preferred_element_type=F32).astype(BF16)
        out[i] = rows[:32]
        out[8 + i] = rows[32:]


def call(kernel, out_shapes, scratch, args, smem=0, hbm=0, sems=0, flops=0):
    specs = [pl.BlockSpec(memory_space=pltpu.SMEM)] * smem
    specs += [pl.BlockSpec(memory_space=pltpu.HBM)] * hbm
    specs += [pl.BlockSpec(memory_space=pltpu.VMEM)] * (len(args) - smem - hbm)
    shapes = [pltpu.VMEM(s, t) for s, t in scratch]
    if sems:
        shapes.append(pltpu.SemaphoreType.DMA((sems,)))
    return pl.pallas_call(
        kernel,
        out_shape=[jax.ShapeDtypeStruct(s, t) for s, t in out_shapes],
        in_specs=specs,
        out_specs=[pl.BlockSpec(memory_space=pltpu.VMEM)] * len(out_shapes),
        scratch_shapes=shapes,
        compiler_params=pltpu.CompilerParams(vmem_limit_bytes=VMEM_LIMIT),
        cost_estimate=pl.CostEstimate(flops=flops, bytes_accessed=4 * 2**20, transcendentals=0),
    )(*args)


def build_tables(rel):
    hot0, code0 = near_patterns()
    hot1, code1 = far_patterns()
    return call(
        table_kernel,
        [((2, 2, GROUP * 64, 256), F32), ((2, GROUP * 64, 256), F32)],
        [],
        [rel, bf(hot0), jnp.asarray(code0), bf(hot1), jnp.asarray(code1)],
        flops=3 * 10**9,
    )


def near_call(pos, fmap, wconv, wqkv, wout, up, down, left, right, bconv, gain0, shift0, gains, shifts, bqkv, table, bout):
    krow, kcol = near_keys()
    rows = np.repeat(np.arange(4) * 4, 2)[:, None] + np.tile(krow, (4, 1)) - 3
    cols = np.tile(np.arange(2) * 16, 4)[:, None] + np.tile(kcol, (4, 1)) - 3
    tok = ((PAIRS, PT, C3), BF16)
    (x1,) = call(
        near_kernel,
        [((512, C3), BF16)],
        [
            ((NTOK, 9 * C2), BF16), tok, tok, tok, tok, ((512, C3), BF16), ((512, C3), F32),
            ((512, C3), BF16), ((512, C3), BF16), ((32, 64, C2), BF16), ((9 * C2, C3), BF16),
            ((C3, 3 * C3), BF16), ((C3, C3), BF16), ((512, 512), BF16), ((8, 256), F32),
        ],
        [
            pos, fmap, wconv.reshape(9 * C2, C3), wqkv, wout, bf(send_matrix()), up, down, left, right,
            bf(pick_matrix()), bconv.reshape(1, C3), gain0.reshape(1, C3), shift0.reshape(1, C3), gains,
            shifts, bqkv, table, jnp.asarray(rows), jnp.asarray(cols), bf(query_matrix()), bout,
        ],
        smem=1, hbm=5, sems=5, flops=10**10,
    )
    return x1


def far_call(pos, wqkv, wout, above, got, below, gains, shifts, bqkv, table, bout):
    (x2,) = call(
        far_kernel,
        [((512, C3), BF16)],
        [
            ((768, C3), BF16), ((704, C3), BF16), ((704, C3), BF16), ((704, C3), BF16),
            ((512, C3), BF16), ((512, C3), BF16), ((C3, 3 * C3), BF16), ((C3, C3), BF16),
        ],
        [pos, wqkv, wout, above, got, below, gains, shifts, bqkv, bf(far_key_matrix()), table, bout],
        smem=1, hbm=2, sems=2, flops=8 * 10**9,
    )
    return x2


def per_device(
    zsize, isize, xsize,
    fmap, wconv, bconv, gain0, shift0, gains, shifts, wqkv, bqkv, rel, wout, bout,
):
    zi, ii, xi = lax.axis_index("gz"), lax.axis_index("gi"), lax.axis_index("gx")
    ysize = zsize * isize
    yi = zi * isize + ii
    pos = jnp.stack([yi, xi, zi, ysize, xsize, zsize]).astype(jnp.int32)

    def shifted(x, dy, dx):
        pairs = [
            (y * xsize + c, ((y + dy) % ysize) * xsize + (c + dx) % xsize)
            for y in range(ysize)
            for c in range(xsize)
        ]
        return lax.ppermute(x, ("gz", "gi", "gx"), pairs)

    up = shifted(fmap[25:], 1, 0)
    down = shifted(fmap[:6], -1, 0)
    table0, table1 = build_tables(rel)

    def strip(at):
        return jnp.concatenate([up[:, at], fmap[:, at], down[:, at]], axis=0)

    left = shifted(strip(slice(56, 64)), 0, 1)
    right = shifted(strip(slice(0, 8)), 0, -1)
    x1 = near_call(
        pos, fmap, wconv, wqkv, wout, up, down, left, right, bconv, gain0, shift0, gains, shifts, bqkv,
        table0, bout,
    )
    got = lax.all_to_all(x1.reshape(64, 8, C3), ("gi", "gx"), 0, 0).reshape(512, C3)
    above = shifted(got[384:], isize, 0)
    below = shifted(got[:128], -isize, 0)
    x2 = far_call(pos, wqkv, wout, above, got, below, gains, shifts, bqkv, table1, bout)
    back = lax.all_to_all(x2.reshape(64, 8, C3), ("gi", "gx"), 0, 0).reshape(512, C3)
    (out,) = call(back_kernel, [((TR, TC, C3), BF16)], [], [back, bf(back_matrix())], flops=10**8)
    return out


def solution(mesh):
    gy, gx = mesh.shape["gy"], mesh.shape["gx"]
    inner = Mesh(mesh.devices.reshape(gy // 8, 8, gx), ("gz", "gi", "gx"))
    tile = P(("gz", "gi"), "gx", None)
    placed = (tile,) + (P(),) * 11
    return jax.shard_map(
        functools.partial(per_device, gy // 8, 8, gx),
        mesh=inner,
        in_specs=placed,
        out_specs=tile,
        check_vma=False,
    )
```

```python
import functools

import jax
import jax.numpy as jnp
import ml_dtypes
import numpy as np
from jax import lax
from jax.experimental import pallas as pl
from jax.experimental.pallas import tpu as pltpu
from jax.sharding import Mesh, PartitionSpec as P

F32 = jnp.float32
BF16 = jnp.bfloat16
KERNEL = 7
HALF = 3
NEG = -1e30
LOG2E = 1.4426950408889634
TR, TC = 16, 32
C2, C3 = 256, 512
HEADS, HD = 16, 32
GROUP = 8
DIL = 8
PAIRS = 11
PT = 80
NTOK = PAIRS * PT
EPS = 1e-5
VMEM_TABLE, VMEM_NEAR, VMEM_FAR, VMEM_BACK = 56, 48, 46, 46


def pair_slots():
    out = []
    for rp in range(2):
        for c in range(16):
            out.append((rp * 16 + c, rp, c))
        for c in range(16, 22):
            out.append((32 + rp * 8 + c - 16, rp, c))
        for c in range(22, 38):
            out.append((48 + rp * 16 + c - 22, rp, c))
    return out


def pick_matrix():
    pick = np.zeros((3 * PT, 160), np.float32)
    for b in range(3):
        for slot, rp, c in pair_slots():
            col = 2 * c + b - 7
            if col < 0:
                k = 128 + 16 * rp + col + 8
            elif col < 64:
                k = 64 * rp + col
            else:
                k = 136 + 16 * rp + col - 64
            pick[b * PT + slot, k] = 1
    return pick


def near_keys():
    rows = np.full((2, 256), -99, np.int32)
    cols = np.full((2, 256), -99, np.int32)
    for half in range(2):
        for j in range(5):
            for slot, rp, c in pair_slots():
                at = slot - 32 * half
                if 0 <= at < 48:
                    rows[half, 48 * j + at] = 2 * j + rp
                    cols[half, 48 * j + at] = c - 16 * half
    return rows, cols


def query_matrix():
    rows, cols = near_keys()
    sel = np.zeros((2, 64, 256), np.float32)
    for half in range(2):
        for k in range(256):
            r, c = rows[half, k] - 3, cols[half, k] - 3
            if 0 <= r < 4 and 0 <= c < 16:
                sel[half, r * 16 + c, k] = 1
    return sel


def near_patterns():
    rows, cols = near_keys()
    hot = np.zeros((49, 2, 2, 4, 256), np.float32)
    code = np.zeros((2, 64, 256), np.int32)
    for half in range(2):
        for k in range(256):
            if rows[half, k] < 0:
                continue
            wide = (cols[half, k] < 16) if half == 0 else (cols[half, k] >= 6)
            for q in range(64):
                dr, dc = rows[half, k] - q // 16, cols[half, k] - q % 16
                if 0 <= dr < 7 and 0 <= dc < 7:
                    part = 0 if wide else 1
                    code[half, q, k] = 1 + part
                    hot[dr * 7 + dc, half, part, q // 16, (k - q % 16) % 256] = 1
    return hot.reshape(49, 4096), code


def far_patterns():
    hot = np.zeros((49, 2, 256), np.float32)
    code = np.zeros((64, 256), np.int32)
    for q in range(64):
        gx, a, b = q // 8, q % 8 // 4, q % 4
        for k in range(256):
            dr, dc = k // 32 - a, k % 32 - (4 * gx + b) + 3
            if 0 <= dr < 7 and 0 <= dc < 7:
                code[q, k] = 1
                hot[dr * 7 + dc, a, (k - 4 * gx - 4 * a - b) % 256] = 1
    return hot.reshape(49, 512), code


def send_matrix():
    perm = np.zeros((2, 256, 256), np.float32)
    for m in range(4):
        for h in range(2):
            for qr in range(4):
                for qc in range(16):
                    row, col = 4 * m + qr, 16 * h + qc
                    dst = ((row % 8) * 8 + col % 8) * 8 + (row // 8) * 4 + col // 8
                    src = (m // 2 * 2 + h) * 64 + qr * 16 + qc
                    perm[m % 2, dst - 256 * (m % 2), src] = 1
    return perm


def far_key_matrix():
    sel = np.zeros((64, 128), np.float32)
    for src in range(2):
        for gx in range(8):
            for a in range(2):
                for b in range(4):
                    if (src == 0) == (a == 1):
                        rp = src
                        sel[rp * 32 + gx * 4 + b, src * 64 + gx * 8 + a * 4 + b] = 1
    return sel


def back_matrix():
    sel = np.zeros((64, 64), np.float32)
    for j in range(8):
        for a in range(2):
            for b in range(4):
                sel[a * 32 + b * 8 + j, j * 8 + a * 4 + b] = 1
    return sel


def bf(x):
    return jnp.asarray(x.astype(ml_dtypes.bfloat16))


def norm(v, gain, shift):
    mean = jnp.mean(v, axis=-1, keepdims=True)
    d = v - mean
    var = jnp.mean(d * d, axis=-1, keepdims=True)
    return d * lax.rsqrt(var + EPS) * gain + shift


def attend_block(q, k, v, table, extra):
    lane = lax.broadcasted_iota(jnp.int32, (1, 256), 1) // HD
    outs = []
    for g in range(HEADS // GROUP):
        at = slice(256 * g, 256 * g + 256)
        qg, kg, vg = q[:, at], k[:, at], v[:, at]
        stacked = jnp.concatenate(
            [qg * (lane == h).astype(BF16) for h in range(GROUP)], axis=0
        )
        s = lax.dot_general(stacked, kg, (((1,), (1,)), ((), ())), preferred_element_type=F32)
        s = s + (table(g) if extra is None else table(g) + extra)
        peak = jnp.max(s, axis=-1, keepdims=True)
        p = jnp.exp2(s - peak)
        total = jnp.sum(p, axis=-1, keepdims=True)
        o = jnp.dot(p.astype(BF16), vg, preferred_element_type=F32) * (1.0 / total)
        for w in range(2):
            side = slice(128 * w, 128 * w + 128)
            acc = o[256 * w : 256 * w + 64, side]
            for h in range(1, 4):
                row = 64 * (4 * w + h)
                acc = jnp.where(lane[:, :128] == h, o[row : row + 64, side], acc)
            outs.append(acc)
    return jnp.concatenate(outs, axis=1).astype(BF16)


def project(x, w, bias):
    return jnp.dot(x, w, preferred_element_type=F32) + bias


def scaled(q):
    return (q * (HD**-0.5 * LOG2E)).astype(BF16)


def table_kernel(rel, hot0, code0, hot1, code1, t0, t1):
    def spread(r, hot):
        hi = r.astype(BF16)
        mid = (r - hi.astype(F32)).astype(BF16)
        lo = (r - hi.astype(F32) - mid.astype(F32)).astype(BF16)
        dot = functools.partial(jnp.dot, preferred_element_type=F32)
        return (dot(hi, hot[...]) + dot(mid, hot[...]) + dot(lo, hot[...])) * LOG2E

    e0 = spread(rel[0], hot0)
    e1 = spread(rel[1], hot1)
    for h in range(HEADS):
        for half in range(2):
            for qr in range(4):
                part = []
                for i in range(2):
                    at = ((half * 2 + i) * 4 + qr) * 256
                    one = jnp.broadcast_to(e0[h : h + 1, at : at + 256], (16, 256))
                    part.append(pltpu.roll(one, 0, 1, stride=1, stride_axis=0))
                code = code0[half, 16 * qr : 16 * qr + 16]
                row = h % GROUP * 64 + 16 * qr
                t0[half, h // GROUP, row : row + 16] = jnp.where(
                    code == 1, part[0], jnp.where(code == 2, part[1], NEG)
                )
        two = jnp.concatenate(
            [jnp.broadcast_to(e1[h : h + 1, 256 * a : 256 * a + 256], (4, 256)) for a in range(2)], axis=0
        )
        for gx in range(8):
            row = h % GROUP * 64 + 8 * gx
            t1[h // GROUP, row : row + 8] = jnp.where(
                code1[8 * gx : 8 * gx + 8] == 1, pltpu.roll(two, 4 * gx, 1, stride=1, stride_axis=0), NEG
            )


def start_copies(pairs, sems):
    copies = [pltpu.make_async_copy(src, dst, sems.at[i]) for i, (src, dst) in enumerate(pairs)]
    for copy in copies:
        copy.start()
    return copies


def conv_taps(cat, pick, pairs, main, rim):
    for i, p in enumerate(pairs):
        for a in range(3):
            e0, e1 = 4 * p + a, 4 * p + a + 2
            rows = jnp.concatenate([main(e0), main(e1), rim(e0), rim(e1)], axis=0)
            got = jnp.dot(pick[...], rows, preferred_element_type=F32).astype(BF16)
            for b in range(3):
                at = 256 * (3 * a + b)
                cat[PT * i : PT * i + PT, at : at + 256] = got[PT * b : PT * b + PT]


def rim_mask(pos):
    edge = jnp.where(pos[1] == 0, 0.0, 1.0)
    return jnp.where(lax.broadcasted_iota(jnp.int32, (16, C2), 0) < 8, edge, 1.0).astype(BF16)


def near_inside(pos, krow, kcol):
    rows, cols = krow[...] + pos[0] * TR, kcol[...] + pos[1] * TC
    inside = (rows >= 0) & (rows < pos[3] * TR) & (cols >= 0) & (cols < pos[4] * TC)
    return jnp.where(inside, 0.0, NEG)


def window(ref, first, h):
    part = ref[first : first + 5, 32 * h : 32 * h + 48, :].reshape(240, C3)
    return jnp.concatenate([part, part[:16]], axis=0)


def tokens_of(cat, wconv, wqkv, bconv, gain0, shift0, gains, shifts, bqkv):
    x0 = norm(project(cat, wconv[...], bconv[...]), gain0[...], shift0[...]).astype(BF16)
    y = norm(x0.astype(F32), gains[0:1], shifts[0:1]).astype(BF16)
    kv = project(y, wqkv[:, C3:], bqkv[0:1, C3:]).astype(BF16)
    return [t.reshape(-1, PT, C3) for t in (x0, y, kv[:, :C3], kv[:, C3:])]


def near_rows(firsts, blocks, x0, y, k, v, qsel, table, extra, wqkv, wout, bqkv, bout):
    yq, xq = [], []
    for first in firsts:
        for h in range(2):
            yq.append(jnp.dot(qsel[h], window(y, first, h), preferred_element_type=F32).astype(BF16))
            xq.append(jnp.dot(qsel[h], window(x0, first, h), preferred_element_type=F32))
    q = scaled(project(jnp.concatenate(yq, axis=0), wqkv[:, :C3], bqkv[0:1, :C3]))
    att = []
    for i, block in enumerate(blocks):
        first, h = firsts[i // 2], i % 2
        att.append(
            attend_block(
                q[64 * i : 64 * i + 64], window(k, first, h), window(v, first, h), lambda g: table[h, g],
                extra[block : block + 1],
            )
        )
    out = project(jnp.concatenate(att, axis=0), wout[...], bout[0:1]) + jnp.concatenate(xq, axis=0)
    return out.astype(BF16)


def near_first(
    pos, own_hbm, wconv_hbm, wqkv_hbm, wout_hbm, table_hbm, left, right, pick, bconv, gain0, shift0, gains,
    shifts, bqkv, bout, krow, kcol, qsel, x0s, ys, ks, vs, x1, cat, own, wconv, wqkv, wout, table, sems,
):
    copies = start_copies(
        (
            (own_hbm, own), (wconv_hbm, wconv), (wqkv_hbm.at[0], wqkv), (table_hbm, table),
            (wout_hbm.at[0], wout),
        ),
        sems,
    )
    mask = rim_mask(pos)
    extra = near_inside(pos, krow, kcol)
    copies[0].wait()

    def rim(e):
        return jnp.concatenate([left[e - 7], right[e - 7]], axis=0) * mask

    conv_taps(cat, pick, range(2, 9), lambda e: own[e - 7], rim)
    copies[1].wait()
    copies[2].wait()
    made = tokens_of(cat[...], wconv, wqkv, bconv, gain0, shift0, gains, shifts, bqkv)
    for ref, t in zip((x0s, ys, ks, vs), made):
        ref[...] = t
    copies[3].wait()
    copies[4].wait()
    x1[...] = near_rows(
        (0, 2), (2, 3, 4, 5), x0s, ys, ks, vs, qsel, table, extra, wqkv, wout, bqkv, bout
    )


def near_second(
    pos, own_hbm, wconv_hbm, wqkv_hbm, wout_hbm, table_hbm, up, down, left, right, x0s, ys, ks, vs, x1mid,
    pick, bconv, gain0, shift0, gains, shifts, bqkv, bout, krow, kcol, qsel, send, out, cat, x0b, yb, kb, vb,
    own, wconv, wqkv, wout, table, sems,
):
    held = [
        (src.at[4 * n : 4 * n + 3], dst.at[2 + 3 * n : 5 + 3 * n])
        for src, dst in ((x0s, x0b), (ys, yb), (ks, kb), (vs, vb))
        for n in range(2)
    ]
    copies = start_copies(
        [
            (own_hbm.at[0:2], own.at[0:2]), (own_hbm.at[29:32], own.at[2:5]), (wconv_hbm, wconv),
            (wqkv_hbm.at[0], wqkv), (table_hbm, table), (wout_hbm.at[0], wout),
        ]
        + held,
        sems,
    )
    top = jnp.where(pos[0] == 0, 0.0, 1.0).astype(BF16)
    mask = rim_mask(pos)
    extra = near_inside(pos, krow, kcol)
    copies[0].wait()
    copies[1].wait()

    def main(e):
        if e < 7:
            row = up[e][:64]
            return row * top if e == 6 else row
        if e >= 39:
            return down[e - 39][:64]
        return own[e - 7] if e < 9 else own[e - 7 - 27]

    def rim(e):
        if 7 <= e < 39:
            return jnp.concatenate([left[e - 7], right[e - 7]], axis=0) * mask
        row = (up[e] if e < 7 else down[e - 39])[64:] * mask
        return row * top if e == 6 else row

    conv_taps(cat, pick, (0, 1, 9, 10), main, rim)
    copies[2].wait()
    copies[3].wait()
    made = tokens_of(cat[...], wconv, wqkv, bconv, gain0, shift0, gains, shifts, bqkv)
    for ref, t in zip((x0b, yb, kb, vb), made):
        ref[0:2] = t[:2]
        ref[8:10] = t[2:]
    for copy in copies[4:]:
        copy.wait()
    outer = near_rows(
        (0, 5), (0, 1, 6, 7), x0b, yb, kb, vb, qsel, table, extra, wqkv, wout, bqkv, bout
    )
    mid = x1mid[...]
    for half, src in enumerate(
        (jnp.concatenate([outer[:128], mid[128:]], axis=0), jnp.concatenate([mid[:128], outer[128:]], axis=0))
    ):
        out[256 * half : 256 * half + 256] = jnp.dot(
            send[half], src, preferred_element_type=F32
        ).astype(BF16)


def far_first(
    pos, wqkv_hbm, wout_hbm, got, gains, shifts, bqkv, ksel, table, bout, ka, va, qs, ends, done, ys, yk,
    wqkv, wout, sems,
):
    copies = start_copies(((wqkv_hbm.at[1], wqkv), (wout_hbm.at[1], wout)), sems)
    ys[...] = norm(got[...].astype(F32), gains[1:2], shifts[1:2]).astype(BF16)
    for j in range(7):
        yk[64 * j : 64 * j + 64] = jnp.dot(
            ksel[...], ys[64 * j : 64 * j + 128], preferred_element_type=F32
        ).astype(BF16)
    ends[0:64] = ys[0:64]
    ends[64:128] = ys[448:512]
    copies[0].wait()
    kv = project(yk[...], wqkv[:, C3:], bqkv[1:2, C3:])
    ka[...] = kv[:, :C3].astype(BF16)
    va[...] = kv[:, C3:].astype(BF16)
    q = scaled(project(ys[...], wqkv[:, :C3], bqkv[1:2, :C3]))
    qs[0:128] = q[0:128]
    qs[128:256] = q[384:512]
    outs = []
    for m in range(2, 6):
        keys = slice(64 * (m - 2), 64 * (m - 2) + 256)
        outs.append(attend_block(q[64 * m : 64 * m + 64], ka[keys], va[keys], lambda g: table[g], None))
    copies[1].wait()
    x2 = project(jnp.concatenate(outs, axis=0), wout[...], bout[1:2])
    done[...] = (x2 + got[128:384].astype(F32)).astype(BF16)


def far_second(
    pos, wqkv_hbm, wout_hbm, above, below, got, ka, va, qs, ends, done, gains, shifts, bqkv, ksel, table,
    bout, out, yk, wkv, wout, sems,
):
    copies = start_copies(((wqkv_hbm.at[1, :, C3:], wkv), (wout_hbm.at[1], wout)), sems)
    zi, zsize = pos[2], pos[5]
    out[128:384] = done[...]

    def y_of(ref):
        return norm(ref[...].astype(F32), gains[1:2], shifts[1:2]).astype(BF16)

    over = jnp.concatenate([y_of(above), ends[0:64]], axis=0)
    under = jnp.concatenate([ends[64:128], y_of(below)], axis=0)
    for j in range(4):
        rows = (over if j < 2 else under)[64 * (j % 2) : 64 * (j % 2) + 128]
        yk[64 * j : 64 * j + 64] = jnp.dot(ksel[...], rows, preferred_element_type=F32).astype(BF16)
    copies[0].wait()
    kv = project(yk[...], wkv[...], bqkv[1:2, C3:]).astype(BF16)
    key_row = lax.broadcasted_iota(jnp.int32, (1, 256), 1) // 32 - 3
    outs = []
    for i, m in enumerate((0, 1, 6, 7)):
        row = key_row + (16 * zi + 2 * m)
        extra = jnp.where((row >= 0) & (row < 16 * zsize), 0.0, NEG)

        def keys(fresh, held):
            parts = (
                [fresh[0:128], held[0:128]], [fresh[64:128], held[0:192]],
                [held[256:448], fresh[128:192]], [held[320:448], fresh[128:256]],
            )[i]
            return jnp.concatenate(parts, axis=0)

        k, v = keys(kv[:, :C3], ka), keys(kv[:, C3:], va)
        outs.append(attend_block(qs[64 * i : 64 * i + 64], k, v, lambda g: table[g], extra))
    copies[1].wait()
    x2 = project(jnp.concatenate(outs, axis=0), wout[...], bout[1:2])
    out[0:128] = (x2[0:128] + got[0:128].astype(F32)).astype(BF16)
    out[384:512] = (x2[128:256] + got[384:512].astype(F32)).astype(BF16)


def back_kernel(got, sel, out):
    for i in range(8):
        rows = jnp.dot(sel[...], got[64 * i : 64 * i + 64], preferred_element_type=F32).astype(BF16)
        out[i] = rows[:32]
        out[8 + i] = rows[32:]


def call(kernel, out_shapes, scratch, args, smem=0, hbm=0, sems=0, flops=0, vmem=VMEM_NEAR):
    specs = [pl.BlockSpec(memory_space=pltpu.SMEM)] * smem
    specs += [pl.BlockSpec(memory_space=pltpu.HBM)] * hbm
    specs += [pl.BlockSpec(memory_space=pltpu.VMEM)] * (len(args) - smem - hbm)
    shapes = [pltpu.VMEM(s, t) for s, t in scratch]
    if sems:
        shapes.append(pltpu.SemaphoreType.DMA((sems,)))
    return pl.pallas_call(
        kernel,
        out_shape=[jax.ShapeDtypeStruct(s, t) for s, t in out_shapes],
        in_specs=specs,
        out_specs=[pl.BlockSpec(memory_space=pltpu.VMEM)] * len(out_shapes),
        scratch_shapes=shapes,
        compiler_params=pltpu.CompilerParams(vmem_limit_bytes=vmem * 2**20),
        cost_estimate=pl.CostEstimate(flops=flops, bytes_accessed=4 * 2**20, transcendentals=0),
    )(*args)


def build_tables(rel):
    hot0, code0 = near_patterns()
    hot1, code1 = far_patterns()
    return call(
        table_kernel,
        [((2, 2, GROUP * 64, 256), F32), ((2, GROUP * 64, 256), F32)],
        [],
        [rel, bf(hot0), jnp.asarray(code0), bf(hot1), jnp.asarray(code1)],
        flops=3 * 10**9, vmem=VMEM_TABLE,
    )


def near_consts():
    krow, kcol = near_keys()
    rows = np.repeat(np.arange(4) * 4, 2)[:, None] + np.tile(krow, (4, 1)) - 3
    cols = np.tile(np.arange(2) * 16, 4)[:, None] + np.tile(kcol, (4, 1)) - 3
    return [jnp.asarray(rows), jnp.asarray(cols), bf(query_matrix())]


def tall(n):
    return ((n, C3), BF16)


INNER = ((7, PT, C3), BF16)
WEIGHTS = [((9 * C2, C3), BF16), ((C3, 3 * C3), BF16)]
NEAR_COPIES = WEIGHTS + [tall(C3), ((2, 2, GROUP * 64, 256), F32)]


def near_first_call(pos, fmap, wconv, wqkv, wout, table, left, right, vecs):
    return call(
        near_first,
        [INNER, INNER, INNER, INNER, tall(256)],
        [((7 * PT, 9 * C2), BF16), ((32, 64, C2), BF16)] + NEAR_COPIES,
        [
            pos, fmap, wconv, wqkv, wout, table, left, right, bf(pick_matrix()), *vecs, *near_consts(),
        ],
        smem=1, hbm=5, sems=5, flops=8 * 10**9,
    )


def near_second_call(pos, fmap, wconv, wqkv, wout, table, up, down, left, right, first, vecs):
    part = ((10, PT, C3), BF16)
    (x1,) = call(
        near_second,
        [tall(512)],
        [((4 * PT, 9 * C2), BF16), part, part, part, part, ((5, 64, C2), BF16)] + NEAR_COPIES,
        [
            pos, fmap, wconv, wqkv, wout, table, up, down, left, right, *first, bf(pick_matrix()), *vecs,
            *near_consts(), bf(send_matrix()),
        ],
        smem=1, hbm=5, sems=14, flops=6 * 10**9,
    )
    return x1


def far_first_call(pos, wqkv, wout, got, gains, shifts, bqkv, table, bout):
    return call(
        far_first,
        [tall(448), tall(448), tall(256), tall(128), tall(256)],
        [tall(512), tall(448), WEIGHTS[1], tall(C3)],
        [pos, wqkv, wout, got, gains, shifts, bqkv, bf(far_key_matrix()), table, bout],
        smem=1, hbm=2, sems=2, flops=6 * 10**9, vmem=VMEM_FAR,
    )


def far_second_call(pos, wqkv, wout, above, below, got, first, gains, shifts, bqkv, table, bout):
    (x2,) = call(
        far_second,
        [tall(512)],
        [tall(256), ((C3, 2 * C3), BF16), tall(C3)],
        [
            pos, wqkv, wout, above, below, got, *first, gains, shifts, bqkv, bf(far_key_matrix()), table, bout,
        ],
        smem=1, hbm=2, sems=2, flops=4 * 10**9, vmem=VMEM_FAR,
    )
    return x2


def per_device(
    zsize, isize, xsize,
    fmap, wconv, bconv, gain0, shift0, gains, shifts, wqkv, bqkv, rel, wout, bout,
):
    zi, ii, xi = lax.axis_index("gz"), lax.axis_index("gi"), lax.axis_index("gx")
    ysize = zsize * isize
    yi = zi * isize + ii
    pos = jnp.stack([yi, xi, zi, ysize, xsize, zsize]).astype(jnp.int32)

    def shifted(x, dy, dx):
        pairs = [
            (y * xsize + c, ((y + dy) % ysize) * xsize + (c + dx) % xsize)
            for y in range(ysize)
            for c in range(xsize)
        ]
        return lax.ppermute(x, ("gz", "gi", "gx"), pairs)

    row = lambda v: v.reshape(1, C3)
    left, right = shifted(fmap[:, 56:], 0, 1), shifted(fmap[:, :8], 0, -1)
    table0, table1 = build_tables(rel)
    wconv = wconv.reshape(9 * C2, C3)
    vecs = [row(bconv), row(gain0), row(shift0), gains, shifts, bqkv, bout]

    def strip(at):
        return jnp.concatenate([fmap[at], left[at], right[at]], axis=1)

    up, down = shifted(strip(slice(25, 32)), 1, 0), shifted(strip(slice(0, 6)), -1, 0)
    first = near_first_call(pos, fmap, wconv, wqkv, wout, table0, left, right, vecs)
    x1 = near_second_call(pos, fmap, wconv, wqkv, wout, table0, up, down, left, right, first, vecs)
    got = lax.all_to_all(x1.reshape(64, 8, C3), ("gi", "gx"), 0, 0).reshape(512, C3)
    above = shifted(got[384:], isize, 0)
    below = shifted(got[:128], -isize, 0)
    first = far_first_call(pos, wqkv, wout, got, gains, shifts, bqkv, table1, bout)
    x2 = far_second_call(pos, wqkv, wout, above, below, got, first, gains, shifts, bqkv, table1, bout)
    back = lax.all_to_all(x2.reshape(64, 8, C3), ("gi", "gx"), 0, 0).reshape(512, C3)
    (out,) = call(back_kernel, [((TR, TC, C3), BF16)], [], [back, bf(back_matrix())], flops=10**8, vmem=VMEM_BACK)
    return out


def solution(mesh):
    gy, gx = mesh.shape["gy"], mesh.shape["gx"]
    inner = Mesh(mesh.devices.reshape(gy // 8, 8, gx), ("gz", "gi", "gx"))
    tile = P(("gz", "gi"), "gx", None)
    placed = (tile,) + (P(),) * 11
    return jax.shard_map(
        functools.partial(per_device, gy // 8, 8, gx),
        mesh=inner,
        in_specs=placed,
        out_specs=tile,
        check_vma=False,
    )
```

```python
import functools

import jax
import jax.numpy as jnp
import ml_dtypes
import numpy as np
from jax import lax
from jax.experimental import pallas as pl
from jax.experimental.pallas import tpu as pltpu
from jax.sharding import Mesh, PartitionSpec as P

F32 = jnp.float32
BF16 = jnp.bfloat16
KERNEL = 7
HALF = 3
NEG = -1e30
LOG2E = 1.4426950408889634
TR, TC = 16, 32
C2, C3 = 256, 512
HEADS, HD = 16, 32
GROUP = 8
DIL = 8
PAIRS = 11
PT = 80
NTOK = PAIRS * PT
EPS = 1e-5
VMEM_TABLE, VMEM_NEAR, VMEM_FAR, VMEM_BACK = 56, 39, 46, 46


def pair_slots():
    out = []
    for rp in range(2):
        for c in range(16):
            out.append((rp * 16 + c, rp, c))
        for c in range(16, 22):
            out.append((32 + rp * 8 + c - 16, rp, c))
        for c in range(22, 38):
            out.append((48 + rp * 16 + c - 22, rp, c))
    return out


def pick_matrix():
    pick = np.zeros((3 * PT, 160), np.float32)
    for b in range(3):
        for slot, rp, c in pair_slots():
            col = 2 * c + b - 7
            if col < 0:
                k = 128 + 16 * rp + col + 8
            elif col < 64:
                k = 64 * rp + col
            else:
                k = 136 + 16 * rp + col - 64
            pick[b * PT + slot, k] = 1
    return pick


def near_keys():
    rows = np.full((2, 256), -99, np.int32)
    cols = np.full((2, 256), -99, np.int32)
    for half in range(2):
        for j in range(5):
            for slot, rp, c in pair_slots():
                at = slot - 32 * half
                if 0 <= at < 48:
                    rows[half, 48 * j + at] = 2 * j + rp
                    cols[half, 48 * j + at] = c - 16 * half
    return rows, cols


def query_matrix():
    rows, cols = near_keys()
    sel = np.zeros((2, 64, 256), np.float32)
    for half in range(2):
        for k in range(256):
            r, c = rows[half, k] - 3, cols[half, k] - 3
            if 0 <= r < 4 and 0 <= c < 16:
                sel[half, r * 16 + c, k] = 1
    return sel


def near_patterns():
    rows, cols = near_keys()
    hot = np.zeros((49, 2, 2, 4, 256), np.float32)
    code = np.zeros((2, 64, 256), np.int32)
    for half in range(2):
        for k in range(256):
            if rows[half, k] < 0:
                continue
            wide = (cols[half, k] < 16) if half == 0 else (cols[half, k] >= 6)
            for q in range(64):
                dr, dc = rows[half, k] - q // 16, cols[half, k] - q % 16
                if 0 <= dr < 7 and 0 <= dc < 7:
                    part = 0 if wide else 1
                    code[half, q, k] = 1 + part
                    hot[dr * 7 + dc, half, part, q // 16, (k - q % 16) % 256] = 1
    return hot.reshape(49, 4096), code


def far_patterns():
    hot = np.zeros((49, 2, 256), np.float32)
    code = np.zeros((64, 256), np.int32)
    for q in range(64):
        gx, a, b = q // 8, q % 8 // 4, q % 4
        for k in range(256):
            dr, dc = k // 32 - a, k % 32 - (4 * gx + b) + 3
            if 0 <= dr < 7 and 0 <= dc < 7:
                code[q, k] = 1
                hot[dr * 7 + dc, a, (k - 4 * gx - 4 * a - b) % 256] = 1
    return hot.reshape(49, 512), code


def send_matrix():
    perm = np.zeros((2, 256, 256), np.float32)
    for m in range(4):
        for h in range(2):
            for qr in range(4):
                for qc in range(16):
                    row, col = 4 * m + qr, 16 * h + qc
                    dst = ((row % 8) * 8 + col % 8) * 8 + (row // 8) * 4 + col // 8
                    src = (m // 2 * 2 + h) * 64 + qr * 16 + qc
                    perm[m % 2, dst - 256 * (m % 2), src] = 1
    return perm


def far_key_matrix():
    sel = np.zeros((64, 128), np.float32)
    for src in range(2):
        for gx in range(8):
            for a in range(2):
                for b in range(4):
                    if (src == 0) == (a == 1):
                        rp = src
                        sel[rp * 32 + gx * 4 + b, src * 64 + gx * 8 + a * 4 + b] = 1
    return sel


def back_matrix():
    sel = np.zeros((64, 64), np.float32)
    for j in range(8):
        for a in range(2):
            for b in range(4):
                sel[a * 32 + b * 8 + j, j * 8 + a * 4 + b] = 1
    return sel


def bf(x):
    return jnp.asarray(x.astype(ml_dtypes.bfloat16))


def norm(v, gain, shift):
    mean = jnp.mean(v, axis=-1, keepdims=True)
    d = v - mean
    var = jnp.mean(d * d, axis=-1, keepdims=True)
    return d * lax.rsqrt(var + EPS) * gain + shift


def attend_block(q, k, v, table, extra):
    lane = lax.broadcasted_iota(jnp.int32, (1, 256), 1) // HD
    outs = []
    for g in range(HEADS // GROUP):
        at = slice(256 * g, 256 * g + 256)
        qg, kg, vg = q[:, at], k[:, at], v[:, at]
        stacked = jnp.concatenate(
            [qg * (lane == h).astype(BF16) for h in range(GROUP)], axis=0
        )
        s = lax.dot_general(stacked, kg, (((1,), (1,)), ((), ())), preferred_element_type=F32)
        s = s + (table(g) if extra is None else table(g) + extra)
        peak = jnp.max(s, axis=-1, keepdims=True)
        p = jnp.exp2(s - peak)
        total = jnp.sum(p, axis=-1, keepdims=True)
        o = jnp.dot(p.astype(BF16), vg, preferred_element_type=F32) * (1.0 / total)
        for w in range(2):
            side = slice(128 * w, 128 * w + 128)
            acc = o[256 * w : 256 * w + 64, side]
            for h in range(1, 4):
                row = 64 * (4 * w + h)
                acc = jnp.where(lane[:, :128] == h, o[row : row + 64, side], acc)
            outs.append(acc)
    return jnp.concatenate(outs, axis=1).astype(BF16)


def project(x, w, bias):
    return jnp.dot(x, w, preferred_element_type=F32) + bias


def scaled(q):
    return (q * (HD**-0.5 * LOG2E)).astype(BF16)


def table_kernel(rel, hot0, code0, hot1, code1, t0, t1):
    def spread(r, hot):
        hi = r.astype(BF16)
        mid = (r - hi.astype(F32)).astype(BF16)
        lo = (r - hi.astype(F32) - mid.astype(F32)).astype(BF16)
        dot = functools.partial(jnp.dot, preferred_element_type=F32)
        return (dot(hi, hot[...]) + dot(mid, hot[...]) + dot(lo, hot[...])) * LOG2E

    e0 = spread(rel[0], hot0)
    e1 = spread(rel[1], hot1)
    for h in range(HEADS):
        for half in range(2):
            for qr in range(4):
                part = []
                for i in range(2):
                    at = ((half * 2 + i) * 4 + qr) * 256
                    one = jnp.broadcast_to(e0[h : h + 1, at : at + 256], (16, 256))
                    part.append(pltpu.roll(one, 0, 1, stride=1, stride_axis=0))
                code = code0[half, 16 * qr : 16 * qr + 16]
                row = h % GROUP * 64 + 16 * qr
                t0[half, h // GROUP, row : row + 16] = jnp.where(
                    code == 1, part[0], jnp.where(code == 2, part[1], NEG)
                )
        two = jnp.concatenate(
            [jnp.broadcast_to(e1[h : h + 1, 256 * a : 256 * a + 256], (4, 256)) for a in range(2)], axis=0
        )
        for gx in range(8):
            row = h % GROUP * 64 + 8 * gx
            t1[h // GROUP, row : row + 8] = jnp.where(
                code1[8 * gx : 8 * gx + 8] == 1, pltpu.roll(two, 4 * gx, 1, stride=1, stride_axis=0), NEG
            )


def start_copies(pairs, sems):
    copies = [pltpu.make_async_copy(src, dst, sems.at[i]) for i, (src, dst) in enumerate(pairs)]
    for copy in copies:
        copy.start()
    return copies


def conv_taps(cat, pick, pairs, main, rim):
    for i, p in enumerate(pairs):
        for a in range(3):
            e0, e1 = 4 * p + a, 4 * p + a + 2
            rows = jnp.concatenate([main(e0), main(e1), rim(e0), rim(e1)], axis=0)
            got = jnp.dot(pick[...], rows, preferred_element_type=F32).astype(BF16)
            for b in range(3):
                at = 256 * (3 * a + b)
                cat[PT * i : PT * i + PT, at : at + 256] = got[PT * b : PT * b + PT]


def rim_mask(pos):
    edge = jnp.where(pos[1] == 0, 0.0, 1.0)
    return jnp.where(lax.broadcasted_iota(jnp.int32, (16, C2), 0) < 8, edge, 1.0).astype(BF16)


def near_inside(pos, krow, kcol):
    rows, cols = krow[...] + pos[0] * TR, kcol[...] + pos[1] * TC
    inside = (rows >= 0) & (rows < pos[3] * TR) & (cols >= 0) & (cols < pos[4] * TC)
    return jnp.where(inside, 0.0, NEG)


def window(ref, first, h):
    part = ref[first : first + 5, 32 * h : 32 * h + 48, :].reshape(240, C3)
    return jnp.concatenate([part, part[:16]], axis=0)


def outer_window(new, held, first, h):
    at = slice(32 * h, 32 * h + 48)
    parts = [new[0:2, at], held[0:3, at]] if first == 0 else [held[4:7, at], new[2:4, at]]
    parts = [part.reshape(-1, C3) for part in parts]
    return jnp.concatenate(parts + [parts[0][:16]], axis=0)


def tokens_of(cat, wconv, wqkv, bconv, gain0, shift0, gains, shifts, bqkv, copy):
    x0 = norm(project(cat, wconv[...], bconv[...]), gain0[...], shift0[...]).astype(BF16)
    y = norm(x0.astype(F32), gains[0:1], shifts[0:1]).astype(BF16)
    if copy is not None:
        copy.wait()
    kv = project(y, wqkv[:, C3:], bqkv[0:1, C3:]).astype(BF16)
    return [t.reshape(-1, PT, C3) for t in (x0, y, kv[:, :C3], kv[:, C3:])]


def near_rows(firsts, blocks, x0, y, k, v, qsel, table, extra, wqkv, wout, bqkv, bout, copies):
    yq, xq = [], []
    for first in firsts:
        for h in range(2):
            yq.append(jnp.dot(qsel[h], y(first, h), preferred_element_type=F32).astype(BF16))
            xq.append(jnp.dot(qsel[h], x0(first, h), preferred_element_type=F32))
    q = scaled(project(jnp.concatenate(yq, axis=0), wqkv[:, :C3], bqkv[0:1, :C3]))
    att = []
    if len(copies) > 1:
        copies[0].wait()
    for i, block in enumerate(blocks):
        first, h = firsts[i // 2], i % 2
        att.append(
            attend_block(
                q[64 * i : 64 * i + 64], k(first, h), v(first, h), lambda g: table[h, g],
                extra[block : block + 1],
            )
        )
    copies[-1].wait()
    out = project(jnp.concatenate(att, axis=0), wout[...], bout[0:1]) + jnp.concatenate(xq, axis=0)
    return out.astype(BF16)


def near_first(
    pos, own_hbm, wconv_hbm, wqkv_hbm, wout_hbm, table_hbm, left, right, pick, bconv, gain0, shift0, gains,
    shifts, bqkv, bout, krow, kcol, qsel, x0s, ys, ks, vs, x1, wconv, wqkv, table, cat, own, wout, sems,
):
    copies = start_copies(
        (
            (own_hbm, own), (wconv_hbm, wconv), (wqkv_hbm.at[0], wqkv), (table_hbm, table),
            (wout_hbm.at[0], wout),
        ),
        sems,
    )
    mask = rim_mask(pos)
    extra = near_inside(pos, krow, kcol)
    copies[0].wait()

    def rim(e):
        return jnp.concatenate([left[e - 7], right[e - 7]], axis=0) * mask

    conv_taps(cat, pick, range(2, 9), lambda e: own[e - 7], rim)
    copies[1].wait()
    made = tokens_of(cat[...], wconv, wqkv, bconv, gain0, shift0, gains, shifts, bqkv, copies[2])
    for ref, t in zip((x0s, ys, ks, vs), made):
        ref[...] = t
    views = [functools.partial(window, ref) for ref in (x0s, ys, ks, vs)]
    x1[...] = near_rows(
        (0, 2), (2, 3, 4, 5), *views, qsel, table, extra, wqkv, wout, bqkv, bout, copies[3:]
    )


def near_second(
    pos, own_hbm, wout_hbm, up, down, left, right, x0s, ys, ks, vs, x1mid, wconv, wqkv, table, pick, bconv,
    gain0, shift0, gains, shifts, bqkv, bout, krow, kcol, qsel, send, out, cat, x0b, yb, kb, vb, own, wout,
    sems,
):
    copies = start_copies(
        (
            (own_hbm.at[0:2], own.at[0:2]), (own_hbm.at[29:32], own.at[2:5]), (wout_hbm.at[0], wout),
        ),
        sems,
    )
    top = jnp.where(pos[0] == 0, 0.0, 1.0).astype(BF16)
    mask = rim_mask(pos)
    extra = near_inside(pos, krow, kcol)
    copies[0].wait()
    copies[1].wait()

    def main(e):
        if e < 7:
            row = up[e][:64]
            return row * top if e == 6 else row
        if e >= 39:
            return down[e - 39][:64]
        return own[e - 7] if e < 9 else own[e - 7 - 27]

    def rim(e):
        if 7 <= e < 39:
            return jnp.concatenate([left[e - 7], right[e - 7]], axis=0) * mask
        row = (up[e] if e < 7 else down[e - 39])[64:] * mask
        return row * top if e == 6 else row

    conv_taps(cat, pick, (0, 1, 9, 10), main, rim)
    made = tokens_of(cat[...], wconv, wqkv, bconv, gain0, shift0, gains, shifts, bqkv, None)
    for ref, t in zip((x0b, yb, kb, vb), made):
        ref[...] = t
    views = [
        functools.partial(outer_window, new, held)
        for new, held in ((x0b, x0s), (yb, ys), (kb, ks), (vb, vs))
    ]
    outer = near_rows(
        (0, 5), (0, 1, 6, 7), *views, qsel, table, extra, wqkv, wout, bqkv, bout, copies[2:]
    )
    mid = x1mid[...]
    for half, src in enumerate(
        (jnp.concatenate([outer[:128], mid[128:]], axis=0), jnp.concatenate([mid[:128], outer[128:]], axis=0))
    ):
        out[256 * half : 256 * half + 256] = jnp.dot(
            send[half], src, preferred_element_type=F32
        ).astype(BF16)


def far_first(
    pos, wqkv_hbm, wout_hbm, got, gains, shifts, bqkv, ksel, table, bout, ka, va, qs, ends, done, ys, yk,
    wqkv, wout, sems,
):
    copies = start_copies(((wqkv_hbm.at[1], wqkv), (wout_hbm.at[1], wout)), sems)
    ys[...] = norm(got[...].astype(F32), gains[1:2], shifts[1:2]).astype(BF16)
    for j in range(7):
        yk[64 * j : 64 * j + 64] = jnp.dot(
            ksel[...], ys[64 * j : 64 * j + 128], preferred_element_type=F32
        ).astype(BF16)
    ends[0:64] = ys[0:64]
    ends[64:128] = ys[448:512]
    copies[0].wait()
    kv = project(yk[...], wqkv[:, C3:], bqkv[1:2, C3:])
    ka[...] = kv[:, :C3].astype(BF16)
    va[...] = kv[:, C3:].astype(BF16)
    q = scaled(project(ys[...], wqkv[:, :C3], bqkv[1:2, :C3]))
    qs[0:128] = q[0:128]
    qs[128:256] = q[384:512]
    outs = []
    for m in range(2, 6):
        keys = slice(64 * (m - 2), 64 * (m - 2) + 256)
        outs.append(attend_block(q[64 * m : 64 * m + 64], ka[keys], va[keys], lambda g: table[g], None))
    copies[1].wait()
    x2 = project(jnp.concatenate(outs, axis=0), wout[...], bout[1:2])
    done[...] = (x2 + got[128:384].astype(F32)).astype(BF16)


def far_second(
    pos, wqkv_hbm, wout_hbm, above, below, got, ka, va, qs, ends, done, gains, shifts, bqkv, ksel, table,
    bout, out, yk, wkv, wout, sems,
):
    copies = start_copies(((wqkv_hbm.at[1, :, C3:], wkv), (wout_hbm.at[1], wout)), sems)
    zi, zsize = pos[2], pos[5]
    out[128:384] = done[...]

    def y_of(ref):
        return norm(ref[...].astype(F32), gains[1:2], shifts[1:2]).astype(BF16)

    over = jnp.concatenate([y_of(above), ends[0:64]], axis=0)
    under = jnp.concatenate([ends[64:128], y_of(below)], axis=0)
    for j in range(4):
        rows = (over if j < 2 else under)[64 * (j % 2) : 64 * (j % 2) + 128]
        yk[64 * j : 64 * j + 64] = jnp.dot(ksel[...], rows, preferred_element_type=F32).astype(BF16)
    copies[0].wait()
    kv = project(yk[...], wkv[...], bqkv[1:2, C3:]).astype(BF16)
    key_row = lax.broadcasted_iota(jnp.int32, (1, 256), 1) // 32 - 3
    outs = []
    for i, m in enumerate((0, 1, 6, 7)):
        row = key_row + (16 * zi + 2 * m)
        extra = jnp.where((row >= 0) & (row < 16 * zsize), 0.0, NEG)

        def keys(fresh, held):
            parts = (
                [fresh[0:128], held[0:128]], [fresh[64:128], held[0:192]],
                [held[256:448], fresh[128:192]], [held[320:448], fresh[128:256]],
            )[i]
            return jnp.concatenate(parts, axis=0)

        k, v = keys(kv[:, :C3], ka), keys(kv[:, C3:], va)
        outs.append(attend_block(qs[64 * i : 64 * i + 64], k, v, lambda g: table[g], extra))
    copies[1].wait()
    x2 = project(jnp.concatenate(outs, axis=0), wout[...], bout[1:2])
    out[0:128] = (x2[0:128] + got[0:128].astype(F32)).astype(BF16)
    out[384:512] = (x2[128:256] + got[384:512].astype(F32)).astype(BF16)


def back_kernel(got, sel, out):
    for i in range(8):
        rows = jnp.dot(sel[...], got[64 * i : 64 * i + 64], preferred_element_type=F32).astype(BF16)
        out[i] = rows[:32]
        out[8 + i] = rows[32:]


def call(kernel, out_shapes, scratch, args, smem=0, hbm=0, sems=0, flops=0, vmem=VMEM_NEAR):
    specs = [pl.BlockSpec(memory_space=pltpu.SMEM)] * smem
    specs += [pl.BlockSpec(memory_space=pltpu.HBM)] * hbm
    specs += [pl.BlockSpec(memory_space=pltpu.VMEM)] * (len(args) - smem - hbm)
    shapes = [pltpu.VMEM(s, t) for s, t in scratch]
    if sems:
        shapes.append(pltpu.SemaphoreType.DMA((sems,)))
    return pl.pallas_call(
        kernel,
        out_shape=[jax.ShapeDtypeStruct(s, t) for s, t in out_shapes],
        in_specs=specs,
        out_specs=[pl.BlockSpec(memory_space=pltpu.VMEM)] * len(out_shapes),
        scratch_shapes=shapes,
        compiler_params=pltpu.CompilerParams(vmem_limit_bytes=vmem * 2**20),
        cost_estimate=pl.CostEstimate(flops=flops, bytes_accessed=4 * 2**20, transcendentals=0),
    )(*args)


def build_tables(rel):
    hot0, code0 = near_patterns()
    hot1, code1 = far_patterns()
    return call(
        table_kernel,
        [((2, 2, GROUP * 64, 256), F32), ((2, GROUP * 64, 256), F32)],
        [],
        [rel, bf(hot0), jnp.asarray(code0), bf(hot1), jnp.asarray(code1)],
        flops=3 * 10**9, vmem=VMEM_TABLE,
    )


def near_consts():
    krow, kcol = near_keys()
    rows = np.repeat(np.arange(4) * 4, 2)[:, None] + np.tile(krow, (4, 1)) - 3
    cols = np.tile(np.arange(2) * 16, 4)[:, None] + np.tile(kcol, (4, 1)) - 3
    return [jnp.asarray(rows), jnp.asarray(cols), bf(query_matrix())]


def tall(n):
    return ((n, C3), BF16)


INNER = ((7, PT, C3), BF16)
WEIGHTS = [((9 * C2, C3), BF16), ((C3, 3 * C3), BF16)]
TABLE = ((2, 2, GROUP * 64, 256), F32)


def near_first_call(pos, fmap, wconv, wqkv, wout, table, left, right, vecs):
    return call(
        near_first,
        [INNER, INNER, INNER, INNER, tall(256), *WEIGHTS, TABLE],
        [((7 * PT, 9 * C2), BF16), ((32, 64, C2), BF16), tall(C3)],
        [
            pos, fmap, wconv, wqkv, wout, table, left, right, bf(pick_matrix()), *vecs, *near_consts(),
        ],
        smem=1, hbm=5, sems=5, flops=8 * 10**9,
    )


def near_second_call(pos, fmap, wout, up, down, left, right, first, vecs):
    part = ((4, PT, C3), BF16)
    (x1,) = call(
        near_second,
        [tall(512)],
        [((4 * PT, 9 * C2), BF16), part, part, part, part, ((5, 64, C2), BF16), tall(C3)],
        [
            pos, fmap, wout, up, down, left, right, *first, bf(pick_matrix()), *vecs,
            *near_consts(), bf(send_matrix()),
        ],
        smem=1, hbm=2, sems=3, flops=6 * 10**9,
    )
    return x1


def far_first_call(pos, wqkv, wout, got, gains, shifts, bqkv, table, bout):
    return call(
        far_first,
        [tall(448), tall(448), tall(256), tall(128), tall(256)],
        [tall(512), tall(448), WEIGHTS[1], tall(C3)],
        [pos, wqkv, wout, got, gains, shifts, bqkv, bf(far_key_matrix()), table, bout],
        smem=1, hbm=2, sems=2, flops=6 * 10**9, vmem=VMEM_FAR,
    )


def far_second_call(pos, wqkv, wout, above, below, got, first, gains, shifts, bqkv, table, bout):
    (x2,) = call(
        far_second,
        [tall(512)],
        [tall(256), ((C3, 2 * C3), BF16), tall(C3)],
        [
            pos, wqkv, wout, above, below, got, *first, gains, shifts, bqkv, bf(far_key_matrix()), table, bout,
        ],
        smem=1, hbm=2, sems=2, flops=4 * 10**9, vmem=VMEM_FAR,
    )
    return x2


def per_device(
    zsize, isize, xsize,
    fmap, wconv, bconv, gain0, shift0, gains, shifts, wqkv, bqkv, rel, wout, bout,
):
    zi, ii, xi = lax.axis_index("gz"), lax.axis_index("gi"), lax.axis_index("gx")
    ysize = zsize * isize
    yi = zi * isize + ii
    pos = jnp.stack([yi, xi, zi, ysize, xsize, zsize]).astype(jnp.int32)

    def shifted(x, dy, dx):
        pairs = [
            (y * xsize + c, ((y + dy) % ysize) * xsize + (c + dx) % xsize)
            for y in range(ysize)
            for c in range(xsize)
        ]
        return lax.ppermute(x, ("gz", "gi", "gx"), pairs)

    row = lambda v: v.reshape(1, C3)
    left, right = shifted(fmap[:, 56:], 0, 1), shifted(fmap[:, :8], 0, -1)
    table0, table1 = build_tables(rel)
    wconv = wconv.reshape(9 * C2, C3)
    vecs = [row(bconv), row(gain0), row(shift0), gains, shifts, bqkv, bout]

    def strip(at):
        return jnp.concatenate([fmap[at], left[at], right[at]], axis=1)

    up, down = shifted(strip(slice(25, 32)), 1, 0), shifted(strip(slice(0, 6)), -1, 0)
    first = near_first_call(pos, fmap, wconv, wqkv, wout, table0, left, right, vecs)
    x1 = near_second_call(pos, fmap, wout, up, down, left, right, first, vecs)
    got = lax.all_to_all(x1.reshape(64, 8, C3), ("gi", "gx"), 0, 0).reshape(512, C3)
    above = shifted(got[384:], isize, 0)
    below = shifted(got[:128], -isize, 0)
    first = far_first_call(pos, wqkv, wout, got, gains, shifts, bqkv, table1, bout)
    x2 = far_second_call(pos, wqkv, wout, above, below, got, first, gains, shifts, bqkv, table1, bout)
    back = lax.all_to_all(x2.reshape(64, 8, C3), ("gi", "gx"), 0, 0).reshape(512, C3)
    (out,) = call(back_kernel, [((TR, TC, C3), BF16)], [], [back, bf(back_matrix())], flops=10**8, vmem=VMEM_BACK)
    return out


def solution(mesh):
    gy, gx = mesh.shape["gy"], mesh.shape["gx"]
    inner = Mesh(mesh.devices.reshape(gy // 8, 8, gx), ("gz", "gi", "gx"))
    tile = P(("gz", "gi"), "gx", None)
    placed = (tile,) + (P(),) * 11
    return jax.shard_map(
        functools.partial(per_device, gy // 8, 8, gx),
        mesh=inner,
        in_specs=placed,
        out_specs=tile,
        check_vma=False,
    )
```

```python
import functools

import jax
import jax.numpy as jnp
import ml_dtypes
import numpy as np
from jax import lax
from jax.experimental import pallas as pl
from jax.experimental.pallas import tpu as pltpu
from jax.sharding import Mesh, PartitionSpec as P

F32 = jnp.float32
BF16 = jnp.bfloat16
KERNEL = 7
HALF = 3
NEG = -1e30
LOG2E = 1.4426950408889634
TR, TC = 16, 32
C2, C3 = 256, 512
HEADS, HD = 16, 32
GROUP = 8
DIL = 8
PAIRS = 11
PT = 80
NTOK = PAIRS * PT
EPS = 1e-5
VMEM_TABLE, VMEM_NEAR, VMEM_FAR, VMEM_BACK = 56, 40, 46, 46


def pair_slots():
    out = []
    for rp in range(2):
        for c in range(16):
            out.append((rp * 16 + c, rp, c))
        for c in range(16, 22):
            out.append((32 + rp * 8 + c - 16, rp, c))
        for c in range(22, 38):
            out.append((48 + rp * 16 + c - 22, rp, c))
    return out


def pick_matrix():
    pick = np.zeros((3 * PT, 160), np.float32)
    for b in range(3):
        for slot, rp, c in pair_slots():
            col = 2 * c + b - 7
            if col < 0:
                k = 128 + 16 * rp + col + 8
            elif col < 64:
                k = 64 * rp + col
            else:
                k = 136 + 16 * rp + col - 64
            pick[b * PT + slot, k] = 1
    return pick


def near_keys():
    rows = np.full((2, 256), -99, np.int32)
    cols = np.full((2, 256), -99, np.int32)
    for half in range(2):
        for j in range(5):
            for slot, rp, c in pair_slots():
                at = slot - 32 * half
                if 0 <= at < 48:
                    rows[half, 48 * j + at] = 2 * j + rp
                    cols[half, 48 * j + at] = c - 16 * half
    return rows, cols


def query_matrix():
    rows, cols = near_keys()
    sel = np.zeros((2, 64, 256), np.float32)
    for half in range(2):
        for k in range(256):
            r, c = rows[half, k] - 3, cols[half, k] - 3
            if 0 <= r < 4 and 0 <= c < 16:
                sel[half, r * 16 + c, k] = 1
    return sel


def near_patterns():
    rows, cols = near_keys()
    hot = np.zeros((49, 2, 2, 4, 256), np.float32)
    code = np.zeros((2, 64, 256), np.int32)
    for half in range(2):
        for k in range(256):
            if rows[half, k] < 0:
                continue
            wide = (cols[half, k] < 16) if half == 0 else (cols[half, k] >= 6)
            for q in range(64):
                dr, dc = rows[half, k] - q // 16, cols[half, k] - q % 16
                if 0 <= dr < 7 and 0 <= dc < 7:
                    part = 0 if wide else 1
                    code[half, q, k] = 1 + part
                    hot[dr * 7 + dc, half, part, q // 16, (k - q % 16) % 256] = 1
    return hot.reshape(49, 4096), code


def far_patterns():
    hot = np.zeros((49, 2, 256), np.float32)
    code = np.zeros((64, 256), np.int32)
    for q in range(64):
        gx, a, b = q // 8, q % 8 // 4, q % 4
        for k in range(256):
            dr, dc = k // 32 - a, k % 32 - (4 * gx + b) + 3
            if 0 <= dr < 7 and 0 <= dc < 7:
                code[q, k] = 1
                hot[dr * 7 + dc, a, (k - 4 * gx - 4 * a - b) % 256] = 1
    return hot.reshape(49, 512), code


def send_matrix():
    perm = np.zeros((2, 256, 256), np.float32)
    for m in range(4):
        for h in range(2):
            for qr in range(4):
                for qc in range(16):
                    row, col = 4 * m + qr, 16 * h + qc
                    dst = ((row % 8) * 8 + col % 8) * 8 + (row // 8) * 4 + col // 8
                    src = (m // 2 * 2 + h) * 64 + qr * 16 + qc
                    perm[m % 2, dst - 256 * (m % 2), src] = 1
    return perm


def far_key_matrix():
    sel = np.zeros((64, 128), np.float32)
    for src in range(2):
        for gx in range(8):
            for a in range(2):
                for b in range(4):
                    if (src == 0) == (a == 1):
                        rp = src
                        sel[rp * 32 + gx * 4 + b, src * 64 + gx * 8 + a * 4 + b] = 1
    return sel


def back_matrix():
    sel = np.zeros((64, 64), np.float32)
    for j in range(8):
        for a in range(2):
            for b in range(4):
                sel[a * 32 + b * 8 + j, j * 8 + a * 4 + b] = 1
    return sel


def bf(x):
    return jnp.asarray(x.astype(ml_dtypes.bfloat16))


def norm(v, gain, shift):
    mean = jnp.mean(v, axis=-1, keepdims=True)
    d = v - mean
    var = jnp.mean(d * d, axis=-1, keepdims=True)
    return d * lax.rsqrt(var + EPS) * gain + shift


def attend_block(q, k, v, table, extra):
    lane = lax.broadcasted_iota(jnp.int32, (1, 256), 1) // HD
    outs = []
    for g in range(HEADS // GROUP):
        at = slice(256 * g, 256 * g + 256)
        qg, kg, vg = q[:, at], k[:, at], v[:, at]
        stacked = jnp.concatenate(
            [qg * (lane == h).astype(BF16) for h in range(GROUP)], axis=0
        )
        s = lax.dot_general(stacked, kg, (((1,), (1,)), ((), ())), preferred_element_type=F32)
        s = s + (table(g) if extra is None else table(g) + extra)
        peak = jnp.max(s, axis=-1, keepdims=True)
        p = jnp.exp2(s - peak)
        total = jnp.sum(p, axis=-1, keepdims=True)
        o = jnp.dot(p.astype(BF16), vg, preferred_element_type=F32) * (1.0 / total)
        for w in range(2):
            side = slice(128 * w, 128 * w + 128)
            acc = o[256 * w : 256 * w + 64, side]
            for h in range(1, 4):
                row = 64 * (4 * w + h)
                acc = jnp.where(lane[:, :128] == h, o[row : row + 64, side], acc)
            outs.append(acc)
    return jnp.concatenate(outs, axis=1).astype(BF16)


def project(x, w, bias):
    return jnp.dot(x, w, preferred_element_type=F32) + bias


def scaled(q):
    return (q * (HD**-0.5 * LOG2E)).astype(BF16)


def table_kernel(rel, hot0, code0, hot1, code1, t0, t1):
    def spread(r, hot):
        hi = r.astype(BF16)
        mid = (r - hi.astype(F32)).astype(BF16)
        lo = (r - hi.astype(F32) - mid.astype(F32)).astype(BF16)
        dot = functools.partial(jnp.dot, preferred_element_type=F32)
        return (dot(hi, hot[...]) + dot(mid, hot[...]) + dot(lo, hot[...])) * LOG2E

    e0 = spread(rel[0], hot0)
    e1 = spread(rel[1], hot1)
    for h in range(HEADS):
        for half in range(2):
            for qr in range(4):
                part = []
                for i in range(2):
                    at = ((half * 2 + i) * 4 + qr) * 256
                    one = jnp.broadcast_to(e0[h : h + 1, at : at + 256], (16, 256))
                    part.append(pltpu.roll(one, 0, 1, stride=1, stride_axis=0))
                code = code0[half, 16 * qr : 16 * qr + 16]
                row = h % GROUP * 64 + 16 * qr
                t0[half, h // GROUP, row : row + 16] = jnp.where(
                    code == 1, part[0], jnp.where(code == 2, part[1], NEG)
                )
        two = jnp.concatenate(
            [jnp.broadcast_to(e1[h : h + 1, 256 * a : 256 * a + 256], (4, 256)) for a in range(2)], axis=0
        )
        for gx in range(8):
            row = h % GROUP * 64 + 8 * gx
            t1[h // GROUP, row : row + 8] = jnp.where(
                code1[8 * gx : 8 * gx + 8] == 1, pltpu.roll(two, 4 * gx, 1, stride=1, stride_axis=0), NEG
            )


def start_copies(pairs, sems):
    copies = [pltpu.make_async_copy(src, dst, sems.at[i]) for i, (src, dst) in enumerate(pairs)]
    for copy in copies:
        copy.start()
    return copies


def conv_taps(cat, pick, pairs, main, rim):
    for i, p in enumerate(pairs):
        for a in range(3):
            e0, e1 = 4 * p + a, 4 * p + a + 2
            rows = jnp.concatenate([main(e0), main(e1), rim(e0), rim(e1)], axis=0)
            got = jnp.dot(pick[...], rows, preferred_element_type=F32).astype(BF16)
            for b in range(3):
                at = 256 * (3 * a + b)
                cat[PT * i : PT * i + PT, at : at + 256] = got[PT * b : PT * b + PT]


def rim_mask(pos):
    edge = jnp.where(pos[1] == 0, 0.0, 1.0)
    return jnp.where(lax.broadcasted_iota(jnp.int32, (16, C2), 0) < 8, edge, 1.0).astype(BF16)


def near_inside(pos, krow, kcol):
    rows, cols = krow[...] + pos[0] * TR, kcol[...] + pos[1] * TC
    inside = (rows >= 0) & (rows < pos[3] * TR) & (cols >= 0) & (cols < pos[4] * TC)
    return jnp.where(inside, 0.0, NEG)


def window(ref, first, h):
    part = ref[first : first + 5, 32 * h : 32 * h + 48, :].reshape(240, C3)
    return jnp.concatenate([part, part[:16]], axis=0)


def outer_window(new, held, first, h):
    at = slice(32 * h, 32 * h + 48)
    parts = [new[0:2, at], held[0:3, at]] if first == 0 else [held[4:7, at], new[2:4, at]]
    parts = [part.reshape(-1, C3) for part in parts]
    return jnp.concatenate(parts + [parts[0][:16]], axis=0)


def tokens_of(cat, wconv, wqkv, bconv, gain0, shift0, gains, shifts, bqkv, copy):
    x0 = norm(project(cat, wconv[...], bconv[...]), gain0[...], shift0[...]).astype(BF16)
    y = norm(x0.astype(F32), gains[0:1], shifts[0:1]).astype(BF16)
    if copy is not None:
        copy.wait()
    kv = project(y, wqkv[:, C3:], bqkv[0:1, C3:]).astype(BF16)
    return [t.reshape(-1, PT, C3) for t in (x0, y, kv[:, :C3], kv[:, C3:])]


def near_rows(firsts, blocks, x0, y, k, v, qsel, table, extra, wqkv, wout, bqkv, bout, copies):
    yq, xq = [], []
    for first in firsts:
        for h in range(2):
            yq.append(jnp.dot(qsel[h], y(first, h), preferred_element_type=F32).astype(BF16))
            xq.append(jnp.dot(qsel[h], x0(first, h), preferred_element_type=F32))
    q = scaled(project(jnp.concatenate(yq, axis=0), wqkv[:, :C3], bqkv[0:1, :C3]))
    att = []
    if len(copies) > 1:
        copies[0].wait()
    for i, block in enumerate(blocks):
        first, h = firsts[i // 2], i % 2
        att.append(
            attend_block(
                q[64 * i : 64 * i + 64], k(first, h), v(first, h), lambda g: table[h, g],
                extra[block : block + 1],
            )
        )
    copies[-1].wait()
    out = project(jnp.concatenate(att, axis=0), wout[...], bout[0:1]) + jnp.concatenate(xq, axis=0)
    return out.astype(BF16)


def near_first(
    pos, own_hbm, wconv_hbm, wqkv_hbm, wout_hbm, table_hbm, left, right, pick, bconv, gain0, shift0, gains,
    shifts, bqkv, bout, krow, kcol, qsel, x0s, ys, ks, vs, x1, wconv, wqkv, table, cat, own, wout, sems,
):
    copies = start_copies(
        (
            (own_hbm, own), (wconv_hbm, wconv), (wqkv_hbm.at[0], wqkv), (table_hbm, table),
            (wout_hbm.at[0], wout),
        ),
        sems,
    )
    mask = rim_mask(pos)
    extra = near_inside(pos, krow, kcol)
    copies[0].wait()

    def rim(e):
        return jnp.concatenate([left[e - 7], right[e - 7]], axis=0) * mask

    conv_taps(cat, pick, range(2, 9), lambda e: own[e - 7], rim)
    copies[1].wait()
    made = tokens_of(cat[...], wconv, wqkv, bconv, gain0, shift0, gains, shifts, bqkv, copies[2])
    for ref, t in zip((x0s, ys, ks, vs), made):
        ref[...] = t
    views = [functools.partial(window, ref) for ref in (x0s, ys, ks, vs)]
    x1[...] = near_rows(
        (0, 2), (2, 3, 4, 5), *views, qsel, table, extra, wqkv, wout, bqkv, bout, copies[3:]
    )


def near_second(
    pos, own_hbm, wout_hbm, up, down, left, right, x0s, ys, ks, vs, x1mid, wconv, wqkv, table, pick, bconv,
    gain0, shift0, gains, shifts, bqkv, bout, krow, kcol, qsel, send, out, cat, x0b, yb, kb, vb, own, wout,
    sems,
):
    copies = start_copies(
        (
            (own_hbm.at[0:2], own.at[0:2]), (own_hbm.at[29:32], own.at[2:5]), (wout_hbm.at[0], wout),
        ),
        sems,
    )
    top = jnp.where(pos[0] == 0, 0.0, 1.0).astype(BF16)
    mask = rim_mask(pos)
    extra = near_inside(pos, krow, kcol)
    copies[0].wait()
    copies[1].wait()

    def main(e):
        if e < 7:
            row = up[e][:64]
            return row * top if e == 6 else row
        if e >= 39:
            return down[e - 39][:64]
        return own[e - 7] if e < 9 else own[e - 7 - 27]

    def rim(e):
        if 7 <= e < 39:
            return jnp.concatenate([left[e - 7], right[e - 7]], axis=0) * mask
        row = (up[e] if e < 7 else down[e - 39])[64:] * mask
        return row * top if e == 6 else row

    conv_taps(cat, pick, (0, 1, 9, 10), main, rim)
    made = tokens_of(cat[...], wconv, wqkv, bconv, gain0, shift0, gains, shifts, bqkv, None)
    for ref, t in zip((x0b, yb, kb, vb), made):
        ref[...] = t
    views = [
        functools.partial(outer_window, new, held)
        for new, held in ((x0b, x0s), (yb, ys), (kb, ks), (vb, vs))
    ]
    outer = near_rows(
        (0, 5), (0, 1, 6, 7), *views, qsel, table, extra, wqkv, wout, bqkv, bout, copies[2:]
    )
    mid = x1mid[...]
    for half, src in enumerate(
        (jnp.concatenate([outer[:128], mid[128:]], axis=0), jnp.concatenate([mid[:128], outer[128:]], axis=0))
    ):
        out[256 * half : 256 * half + 256] = jnp.dot(
            send[half], src, preferred_element_type=F32
        ).astype(BF16)


def far_first(
    pos, wqkv_hbm, wout_hbm, got, gains, shifts, bqkv, ksel, table, bout, ka, va, qs, ends, done, ys, yk,
    wqkv, wout, sems,
):
    copies = start_copies(((wqkv_hbm.at[1], wqkv), (wout_hbm.at[1], wout)), sems)
    ys[...] = norm(got[...].astype(F32), gains[1:2], shifts[1:2]).astype(BF16)
    for j in range(7):
        yk[64 * j : 64 * j + 64] = jnp.dot(
            ksel[...], ys[64 * j : 64 * j + 128], preferred_element_type=F32
        ).astype(BF16)
    ends[0:64] = ys[0:64]
    ends[64:128] = ys[448:512]
    copies[0].wait()
    kv = project(yk[...], wqkv[:, C3:], bqkv[1:2, C3:])
    ka[...] = kv[:, :C3].astype(BF16)
    va[...] = kv[:, C3:].astype(BF16)
    q = scaled(project(ys[...], wqkv[:, :C3], bqkv[1:2, :C3]))
    qs[0:128] = q[0:128]
    qs[128:256] = q[384:512]
    outs = []
    for m in range(2, 6):
        keys = slice(64 * (m - 2), 64 * (m - 2) + 256)
        outs.append(attend_block(q[64 * m : 64 * m + 64], ka[keys], va[keys], lambda g: table[g], None))
    copies[1].wait()
    x2 = project(jnp.concatenate(outs, axis=0), wout[...], bout[1:2])
    done[...] = (x2 + got[128:384].astype(F32)).astype(BF16)


def far_second(
    pos, wqkv_hbm, wout_hbm, above, below, got, ka, va, qs, ends, done, gains, shifts, bqkv, ksel, table,
    bout, out, yk, wkv, wout, sems,
):
    copies = start_copies(((wqkv_hbm.at[1, :, C3:], wkv), (wout_hbm.at[1], wout)), sems)
    zi, zsize = pos[2], pos[5]
    out[128:384] = done[...]

    def y_of(ref):
        return norm(ref[...].astype(F32), gains[1:2], shifts[1:2]).astype(BF16)

    over = jnp.concatenate([y_of(above), ends[0:64]], axis=0)
    under = jnp.concatenate([ends[64:128], y_of(below)], axis=0)
    for j in range(4):
        rows = (over if j < 2 else under)[64 * (j % 2) : 64 * (j % 2) + 128]
        yk[64 * j : 64 * j + 64] = jnp.dot(ksel[...], rows, preferred_element_type=F32).astype(BF16)
    copies[0].wait()
    kv = project(yk[...], wkv[...], bqkv[1:2, C3:]).astype(BF16)
    key_row = lax.broadcasted_iota(jnp.int32, (1, 256), 1) // 32 - 3
    outs = []
    for i, m in enumerate((0, 1, 6, 7)):
        row = key_row + (16 * zi + 2 * m)
        extra = jnp.where((row >= 0) & (row < 16 * zsize), 0.0, NEG)

        def keys(fresh, held):
            parts = (
                [fresh[0:128], held[0:128]], [fresh[64:128], held[0:192]],
                [held[256:448], fresh[128:192]], [held[320:448], fresh[128:256]],
            )[i]
            return jnp.concatenate(parts, axis=0)

        k, v = keys(kv[:, :C3], ka), keys(kv[:, C3:], va)
        outs.append(attend_block(qs[64 * i : 64 * i + 64], k, v, lambda g: table[g], extra))
    copies[1].wait()
    x2 = project(jnp.concatenate(outs, axis=0), wout[...], bout[1:2])
    out[0:128] = (x2[0:128] + got[0:128].astype(F32)).astype(BF16)
    out[384:512] = (x2[128:256] + got[384:512].astype(F32)).astype(BF16)


def back_kernel(got, sel, out):
    for i in range(8):
        rows = jnp.dot(sel[...], got[64 * i : 64 * i + 64], preferred_element_type=F32).astype(BF16)
        out[i] = rows[:32]
        out[8 + i] = rows[32:]


def call(kernel, out_shapes, scratch, args, smem=0, hbm=0, sems=0, flops=0, vmem=VMEM_NEAR):
    specs = [pl.BlockSpec(memory_space=pltpu.SMEM)] * smem
    specs += [pl.BlockSpec(memory_space=pltpu.HBM)] * hbm
    specs += [pl.BlockSpec(memory_space=pltpu.VMEM)] * (len(args) - smem - hbm)
    shapes = [pltpu.VMEM(s, t) for s, t in scratch]
    if sems:
        shapes.append(pltpu.SemaphoreType.DMA((sems,)))
    return pl.pallas_call(
        kernel,
        out_shape=[jax.ShapeDtypeStruct(s, t) for s, t in out_shapes],
        in_specs=specs,
        out_specs=[pl.BlockSpec(memory_space=pltpu.VMEM)] * len(out_shapes),
        scratch_shapes=shapes,
        compiler_params=pltpu.CompilerParams(vmem_limit_bytes=vmem * 2**20),
        cost_estimate=pl.CostEstimate(flops=flops, bytes_accessed=4 * 2**20, transcendentals=0),
    )(*args)


def build_tables(rel):
    hot0, code0 = near_patterns()
    hot1, code1 = far_patterns()
    return call(
        table_kernel,
        [((2, 2, GROUP * 64, 256), F32), ((2, GROUP * 64, 256), F32)],
        [],
        [rel, bf(hot0), jnp.asarray(code0), bf(hot1), jnp.asarray(code1)],
        flops=3 * 10**9, vmem=VMEM_TABLE,
    )


def near_consts():
    krow, kcol = near_keys()
    rows = np.repeat(np.arange(4) * 4, 2)[:, None] + np.tile(krow, (4, 1)) - 3
    cols = np.tile(np.arange(2) * 16, 4)[:, None] + np.tile(kcol, (4, 1)) - 3
    return [jnp.asarray(rows), jnp.asarray(cols), bf(query_matrix())]


def tall(n):
    return ((n, C3), BF16)


INNER = ((7, PT, C3), BF16)
WEIGHTS = [((9 * C2, C3), BF16), ((C3, 3 * C3), BF16)]
TABLE = ((2, 2, GROUP * 64, 256), F32)


def near_first_call(pos, fmap, wconv, wqkv, wout, table, left, right, vecs):
    return call(
        near_first,
        [INNER, INNER, INNER, INNER, tall(256), *WEIGHTS, TABLE],
        [((7 * PT, 9 * C2), BF16), ((32, 64, C2), BF16), tall(C3)],
        [
            pos, fmap, wconv, wqkv, wout, table, left, right, bf(pick_matrix()), *vecs, *near_consts(),
        ],
        smem=1, hbm=5, sems=5, flops=8 * 10**9,
    )


def near_second_call(pos, fmap, wout, up, down, left, right, first, vecs):
    part = ((4, PT, C3), BF16)
    (x1,) = call(
        near_second,
        [tall(512)],
        [((4 * PT, 9 * C2), BF16), part, part, part, part, ((5, 64, C2), BF16), tall(C3)],
        [
            pos, fmap, wout, up, down, left, right, *first, bf(pick_matrix()), *vecs,
            *near_consts(), bf(send_matrix()),
        ],
        smem=1, hbm=2, sems=3, flops=6 * 10**9,
    )
    return x1


def far_first_call(pos, wqkv, wout, got, gains, shifts, bqkv, table, bout):
    return call(
        far_first,
        [tall(448), tall(448), tall(256), tall(128), tall(256)],
        [tall(512), tall(448), WEIGHTS[1], tall(C3)],
        [pos, wqkv, wout, got, gains, shifts, bqkv, bf(far_key_matrix()), table, bout],
        smem=1, hbm=2, sems=2, flops=6 * 10**9, vmem=VMEM_FAR,
    )


def far_second_call(pos, wqkv, wout, above, below, got, first, gains, shifts, bqkv, table, bout):
    (x2,) = call(
        far_second,
        [tall(512)],
        [tall(256), ((C3, 2 * C3), BF16), tall(C3)],
        [
            pos, wqkv, wout, above, below, got, *first, gains, shifts, bqkv, bf(far_key_matrix()), table, bout,
        ],
        smem=1, hbm=2, sems=2, flops=4 * 10**9, vmem=VMEM_FAR,
    )
    return x2


def per_device(
    zsize, isize, xsize,
    fmap, wconv, bconv, gain0, shift0, gains, shifts, wqkv, bqkv, rel, wout, bout,
):
    zi, ii, xi = lax.axis_index("gz"), lax.axis_index("gi"), lax.axis_index("gx")
    ysize = zsize * isize
    yi = zi * isize + ii
    pos = jnp.stack([yi, xi, zi, ysize, xsize, zsize]).astype(jnp.int32)

    def shifted(x, dy, dx):
        pairs = [
            (y * xsize + c, ((y + dy) % ysize) * xsize + (c + dx) % xsize)
            for y in range(ysize)
            for c in range(xsize)
        ]
        return lax.ppermute(x, ("gz", "gi", "gx"), pairs)

    row = lambda v: v.reshape(1, C3)
    left, right = shifted(fmap[:, 56:], 0, 1), shifted(fmap[:, :8], 0, -1)
    table0, table1 = build_tables(rel)
    wconv = wconv.reshape(9 * C2, C3)
    vecs = [row(bconv), row(gain0), row(shift0), gains, shifts, bqkv, bout]

    def strip(at):
        return jnp.concatenate([fmap[at], left[at], right[at]], axis=1)

    up, down = shifted(strip(slice(25, 32)), 1, 0), shifted(strip(slice(0, 6)), -1, 0)
    first = near_first_call(pos, fmap, wconv, wqkv, wout, table0, left, right, vecs)
    x1 = near_second_call(pos, fmap, wout, up, down, left, right, first, vecs)
    got = lax.all_to_all(x1.reshape(64, 8, C3), ("gi", "gx"), 0, 0).reshape(512, C3)
    above = shifted(got[384:], isize, 0)
    below = shifted(got[:128], -isize, 0)
    first = far_first_call(pos, wqkv, wout, got, gains, shifts, bqkv, table1, bout)
    x2 = far_second_call(pos, wqkv, wout, above, below, got, first, gains, shifts, bqkv, table1, bout)
    back = lax.all_to_all(x2.reshape(64, 8, C3), ("gi", "gx"), 0, 0).reshape(512, C3)
    (out,) = call(back_kernel, [((TR, TC, C3), BF16)], [], [back, bf(back_matrix())], flops=10**8, vmem=VMEM_BACK)
    return out


def solution(mesh):
    gy, gx = mesh.shape["gy"], mesh.shape["gx"]
    inner = Mesh(mesh.devices.reshape(gy // 8, 8, gx), ("gz", "gi", "gx"))
    tile = P(("gz", "gi"), "gx", None)
    placed = (tile,) + (P(),) * 11
    return jax.shard_map(
        functools.partial(per_device, gy // 8, 8, gx),
        mesh=inner,
        in_specs=placed,
        out_specs=tile,
        check_vma=False,
    )
```
